256 devices in a mesh: rep: 16 (over x, z_hi), grp: 16 (over y, z_lo, core).
Axes of the slice: x: 4, y: 4, z: 8 (z_hi: 4, z_lo: 2; z = z_hi * 2 + z_lo), core: 2. Of those that a mesh axis runs over, the one named last changes fastest.
Arguments:
- owners: int32 [2], replicated, may hold values from 0 to 15, as said below
- store_a: bfloat16 [16, 1024, 1024], P('rep'), may hold values from -0.1875 to 0.1875
- store_g: bfloat16 [16, 4096, 4096], P('rep', 'grp'), may hold values from -0.125 to 0.125
- vals_a: bfloat16 [16, 1024], P('rep'), may hold values from 0.29882812 to 3
- vals_g: bfloat16 [16, 4096], P('rep', 'grp'), may hold values from 0.29882812 to 3
- grads: float32 [2, 1024, 4096], P(None, 'rep', 'grp'), may hold values from -6 to 6
Outputs:
- precond: float32 [2, 1024, 4096], P(None, 'rep', 'grp')
The draws below stay inside these ranges and needn't reach their ends.
Inputs may be any that keep to these rules, and one draw needn't show every extreme that they name: The owners of the 2 layers are distinct indices along rep; index 15 is always among them.
All inputs are finite; a program needn't handle non-finite values.
Results may differ from the reference program's by a relative error of at most 0.0003.
Values may be sent and summed in bfloat16 or wider, within the bound.
A program may use at most 64 MiB of HBM per device.

```python
import math
import jax
import jax.numpy as jnp
from jax import lax

D = 1024
F = 4096
LAYERS = 2
N_REP = 16


def draw_owners(key, part):
    key = jax.random.fold_in(key, 11)
    inner_key = jax.random.fold_in(key, 1)
    order_key = jax.random.fold_in(key, 2)
    others = jax.random.permutation(inner_key, N_REP - 1)
    chosen = jnp.concatenate([jnp.array([N_REP - 1], jnp.int32), others[:LAYERS - 1].astype(jnp.int32)])
    return chosen[jax.random.permutation(order_key, LAYERS)].astype(jnp.int32)


def with_spikes(values, stream_key, source, target, parts, factor):
    owner, partner = [(jnp.arange(values.shape[position]) // (values.shape[position] // parts)).reshape([-1 if axis == position else 1 for axis in range(values.ndim)]) for position in (source, target)]
    chosen = jax.random.permutation(stream_key, parts)[partner]
    strong = (owner == chosen) | (owner == (partner + parts // 2) % parts)
    return jnp.where(strong, factor * values, values)


def steps_of(key, dims, pieces, low, high):
    loudness = 1.0
    for axis_at, blocks in pieces:
        heights = jax.random.uniform(jax.random.fold_in(jax.random.fold_in(key, 6), axis_at), (blocks,), jnp.float32, low / len(pieces), high / len(pieces))
        loudness = loudness * jnp.repeat(jnp.exp(heights), dims[axis_at] // blocks).reshape((-1,) + (1,) * (len(dims) - 1 - axis_at))
    return loudness


def centred(own_key, shape, deviation, reach, split=(), kind=jnp.bfloat16):
    result = deviation * jax.random.normal(own_key, shape, jnp.float32)
    if split:
        result = result * steps_of(own_key, shape, split, -0.22, 0.18)
    return jnp.clip(result, -reach, reach).astype(kind)


def noise_with(own_key, dims, spread, reach, cuts, heavy, kind=jnp.bfloat16):
    values = spread * jax.random.normal(own_key, dims, jnp.float32)
    if cuts:
        values = values * steps_of(own_key, dims, cuts, -0.22, 0.18)
    return jnp.clip(with_spikes(values, jax.random.fold_in(own_key, 3), *heavy), -reach, reach).astype(kind)


def setup_inputs(seed: int = 0) -> dict:
    seeds = jax.random.split(jax.random.key(seed), 7)
    return {
        "owners": draw_owners(jax.random.fold_in(seeds[6], 71), 0),
        "store_a": centred(seeds[1], (N_REP, D, D), D ** -0.5, 0.1875, ((0, 16),)),
        "store_g": noise_with(seeds[2], (N_REP, F, F), F ** -0.5, 0.125, ((0, 16), (1, 16)), (1, 2, 16, 2.0)),
        "vals_a": jnp.clip(jnp.exp(math.log(3.0) - 2.306499 * jax.random.uniform(seeds[3], (N_REP, D), jnp.float32) ** steps_of(seeds[3], (N_REP, D), ((0, 16),), -0.2, 0.2)), 0.29882812, 3.0).astype(jnp.bfloat16),
        "vals_g": jnp.clip(jnp.exp(math.log(3.0) - 2.306499 * jax.random.uniform(seeds[4], (N_REP, F), jnp.float32) ** steps_of(seeds[4], (N_REP, F), ((0, 16), (1, 16)), -0.2, 0.2)), 0.29882812, 3.0).astype(jnp.bfloat16),
        "grads": centred(seeds[5], (LAYERS, D, F), 1.0, 6.0, ((1, 16), (2, 16)), jnp.float32),
    }


DAMPING = 0.1


def product(left, right):
    return jnp.dot(left, right, precision=lax.Precision.HIGHEST, preferred_element_type=jnp.float32)


def reference(owners, store_a, store_g, vals_a, vals_g, grads):
    results = []
    for layer in range(LAYERS):
        holder = owners[layer]
        basis_a = store_a[holder].astype(jnp.float32)
        basis_g = store_g[holder].astype(jnp.float32)
        spec_a = vals_a[holder].astype(jnp.float32)
        spec_g = vals_g[holder].astype(jnp.float32)
        turned = product(grads[layer], basis_g)
        rotated = product(basis_a.T, turned)
        scaled = rotated / (spec_a[:, None] * spec_g[None, :] + DAMPING)
        mixed = product(scaled, basis_g.T)
        results.append(product(basis_a, mixed))
    return jnp.stack(results)
```

```python
import functools

import jax
import jax.numpy as jnp
from jax import lax
from jax.experimental import pallas as pl
from jax.experimental.pallas import tpu as pltpu
from jax.sharding import PartitionSpec as P

DAMPING = 0.1
MESH = pl.DeviceIdType.MESH
NX, NZ, NY, NL, NC = 4, 4, 4, 2, 2
FIXED_OWNER = 15
CHUNKS = 4
BF16, F32 = jnp.bfloat16, jnp.float32


def coords():
    rep, grp = lax.axis_index("rep"), lax.axis_index("grp")
    return rep // NZ, rep % NZ, grp // (NL * NC), (grp // NC) % NL, grp % NC


def dev(x, zh, y, zl, c):
    return (x * NZ + zh, y * (NL * NC) + zl * NC + c)


def greet(peers):
    barrier = pltpu.get_barrier_semaphore()
    for peer in peers:
        pl.semaphore_signal(barrier, inc=1, device_id=peer, device_id_type=MESH)
    pl.semaphore_wait(barrier, len(peers))


def spread_kernel(other, sg, qap, gt, qg, qa, gx, qg_ss, qg_rs, fw_ss, qa_ss, qa_rs, qf_ss, ql_ss, ql_rs, qy_ss, qy_rs,
                  gx_ss, gx_rs, gc_ss, gc_rs, loc):
    x, zh, y, zl, c = coords()
    x_peers = [(x + d) % NX for d in range(1, NX)]
    peers = [dev(p, zh, y, zl, k) for p in x_peers for k in range(NC)]
    peers += [dev(x, zh, y, zl, 1 - c), dev(x, (zh + 1) % NZ, y, zl, c), dev(x, (zh + 3) % NZ, y, zl, c)]
    peers += [dev(x, zh, y, 1 - zl, c)] + [dev(x, zh, (y + d) % NY, zl, c) for d in range(1, NY)]
    greet(peers)

    rows = 256 // CHUNKS
    owners = (FIXED_OWNER, other)
    slot = y * (NL * NC) + zl * NC + c

    def mine(layer):
        return (x == owners[layer] // NZ) & (zh == owners[layer] % NZ)

    def remote(src, dst, ss, rs, to):
        return pltpu.make_async_remote_copy(src_ref=src, dst_ref=dst, send_sem=ss, recv_sem=rs, device_id=to,
                                            device_id_type=MESH)

    def qa_first(layer, d):
        ox, oz = owners[layer] // NZ, owners[layer] % NZ
        return remote(qap, qa.at[slot], qa_ss.at[layer, d], qa_rs.at[c], dev((ox + d) % NX, oz, y, zl, layer))

    def qa_local():
        return pltpu.make_async_copy(qap, qa.at[slot], qa_rs.at[c])

    def qg_first(layer, k, d, core):
        ox, oz = owners[layer] // NZ, owners[layer] % NZ
        tx = (ox + d) % NX
        return remote(sg.at[pl.ds(k * rows, rows), pl.ds((tx * NC + core) * 512, 512)],
                      qg.at[layer, pl.ds(pl.multiple_of(c * 256 + k * rows, rows), rows), :],
                      qg_ss.at[layer, k, d, core], qg_rs.at[layer, c, k], dev(tx, oz, y, zl, core))

    def qg_local(layer, k, core):
        ox = owners[layer] // NZ
        return pltpu.make_async_copy(sg.at[pl.ds(k * rows, rows), pl.ds((ox * NC + core) * 512, 512)],
                                     qg.at[layer, pl.ds(core * 256 + k * rows, rows), :], qg_rs.at[layer, core, k])

    order = (2, 1, 3, 0)
    for layer in range(2):
        @pl.when(mine(layer))
        def _():
            for d in order:
                if d:
                    qa_first(layer, d).start()
                else:
                    @pl.when(c == layer)
                    def _():
                        qa_local().start()

                    @pl.when(c != layer)
                    def _():
                        qa_first(layer, 0).start()

    g_own = [pltpu.make_async_copy(gt.at[l], gx.at[l, pl.ds(pl.multiple_of(x * 64, 64), 64),
                                                   pl.ds(pl.multiple_of(c * 256, 256), 256)], loc.at[l]) for l in range(2)]
    g_x = [[remote(gt.at[l], gx.at[l, pl.ds(pl.multiple_of(x * 64, 64), 64), pl.ds(pl.multiple_of(c * 256, 256), 256)],
                   gx_ss.at[l, d - 1], gx_rs.at[l, d - 1], dev((x + d) % NX, zh, y, zl, c)) for d in range(1, NX)]
           for l in range(2)]
    for l in range(2):
        g_own[l].start()
        for copy in g_x[l]:
            copy.start()

    for k in range(CHUNKS):
        for layer in range(2):
            @pl.when(mine(layer))
            def _():
                for d in order:
                    for core in range(NC):
                        if d:
                            qg_first(layer, k, d, core).start()
                        else:
                            @pl.when(c == core)
                            def _():
                                qg_local(layer, k, core).start()

                            @pl.when(c != core)
                            def _():
                                qg_first(layer, k, 0, core).start()

    def forward(part, layer):
        oz = owners[layer] % NZ
        if part == 0:
            return (zh + 1) % NZ, (zh + NZ - oz) % NZ < NZ - 1
        return (zh + NZ - 1) % NZ, (oz + NZ - zh) % NZ < NZ - 1

    def qa_on(layer, part):
        nxt, _ = forward(part, layer)
        s = y * (NL * NC) + zl * NC + part
        return remote(qa.at[s], qa.at[s], qf_ss.at[part], qa_rs.at[part], dev(x, nxt, y, zl, layer))

    for layer in range(2):
        @pl.when(c == layer)
        def _():
            for part in range(2):
                copy = qa_on(layer, part)
                copy.wait_recv()

                @pl.when(forward(part, layer)[1])
                def _():
                    copy.start()

    two = pl.ds(y * (NL * NC) + zl * NC, NC)
    two_in = pl.ds(y * (NL * NC) + (1 - zl) * NC, NC)
    four = pl.ds(y * (NL * NC), NL * NC)
    qa_l = remote(qa.at[two], qa.at[two], ql_ss, ql_rs, dev(x, zh, y, 1 - zl, c))
    qa_l.start()

    def qg_on(layer, part, k):
        nxt, _ = forward(part, layer)
        block = qg.at[layer, pl.ds(part * 256 + k * rows, rows), :]
        return remote(block, block, fw_ss.at[layer, part, k], qg_rs.at[layer, part, k], dev(x, nxt, y, zl, c))

    def pass_chunk(k):
        for layer in range(2):
            for part in range(2):
                copy = qg_on(layer, part, k)
                copy.wait_recv()

                @pl.when(forward(part, layer)[1])
                def _():
                    copy.start()

    pass_chunk(0)
    g_c = []
    for l in range(2):
        g_own[l].wait()
        for copy in g_x[l]:
            copy.wait_recv()
        half = gx.at[l, :, pl.ds(pl.multiple_of(c * 256, 256), 256)]
        g_c.append(remote(half, half, gc_ss.at[l], gc_rs.at[l], dev(x, zh, y, zl, 1 - c)))
        g_c[l].start()
    qa_l.wait_recv()
    qa_y = [remote(qa.at[four], qa.at[four], qy_ss.at[d - 1], qy_rs.at[d - 1], dev(x, zh, (y + d) % NY, zl, c))
            for d in range(1, NY)]
    for copy in qa_y:
        copy.start()
    for k in range(1, CHUNKS):
        pass_chunk(k)

    for l in range(2):
        g_c[l].wait()
        for copy in g_x[l]:
            copy.wait_send()
    for copy in qa_y:
        copy.wait()
    qa_l.wait_send()
    for layer in range(2):
        for part in range(2):
            @pl.when(forward(part, layer)[1])
            def _():
                @pl.when(c == layer)
                def _():
                    qa_on(layer, part).wait_send()
                for k in range(CHUNKS):
                    qg_on(layer, part, k).wait_send()

        @pl.when(mine(layer))
        def _():
            for d in order:
                if d:
                    qa_first(layer, d).wait_send()
                else:
                    @pl.when(c != layer)
                    def _():
                        qa_first(layer, 0).wait_send()
            for k in range(CHUNKS):
                for d in order:
                    for core in range(NC):
                        if d:
                            qg_first(layer, k, d, core).wait_send()
                        else:
                            @pl.when(c != core)
                            def _():
                                qg_first(layer, k, 0, core).wait_send()


def spread(other, sg, qap, gt):
    dma = pltpu.SemaphoreType.DMA
    anywhere = pl.BlockSpec(memory_space=pl.ANY)
    return pl.pallas_call(
        functools.partial(spread_kernel, other),
        out_shape=(
            jax.ShapeDtypeStruct((2, 512, 512), BF16),
            jax.ShapeDtypeStruct((16, 80, 1024), BF16),
            jax.ShapeDtypeStruct((2, 256, 512), F32),
        ),
        in_specs=[anywhere] * 3,
        out_specs=(anywhere,) * 3,
        scratch_shapes=[
            dma((2, CHUNKS, NX, NC)), dma((2, NC, CHUNKS)), dma((2, 2, CHUNKS)),
            dma((2, NX)), dma((2,)), dma((2,)),
            dma, dma, dma((3,)), dma((3,)),
            dma((2, 3)), dma((2, 3)), dma((2,)), dma((2,)), dma((2,)),
        ],
        compiler_params=pltpu.CompilerParams(collective_id=other, has_side_effects=True),
        name=f"spread_{other}",
    )(sg, qap, gt)


def split(value):
    high = value.astype(BF16)
    low = (value - high.astype(F32)).astype(BF16)
    return jnp.concatenate([high, low], axis=0)


def fold(value):
    half = value.shape[0] // 2
    return value[:half] + value[half:]


def dot(left, right, dims=((1,), (0,))):
    return lax.dot_general(left, right, (dims, ((), ())), preferred_element_type=F32)


def turn_kernel(qg, qa, gx, out, yt, yr, t4, mid, wt, wr, wall, mx, mc, ms, orc, y_ss, y_rs, t_ss, t_rs, w_ss, w_rs, a_ss,
                a_rs, c_ss, c_rs, o_ss, o_rs):
    x, zh, y, zl, c = coords()
    q = y * NL + zl

    def remote(src, dst, ss, rs, to):
        return pltpu.make_async_remote_copy(src_ref=src, dst_ref=dst, send_sem=ss, recv_sem=rs, device_id=to,
                                            device_id_type=MESH)

    near = [((y + dy) % NY, (zl + dl) % NL) for dy in range(NY) for dl in range(NL)]
    peers = [dev(x, zh, ty, tl, k) for ty, tl in near[1:] for k in range(NC)] + [dev(x, zh, y, zl, 1 - c)]
    peers += [dev((x + d) % NX, zh, y, zl, c) for d in range(1, NX)]
    peers += [dev(x, (zh + d) % NZ, y, zl, c) for d in range(1, NZ)]
    greet(peers)

    def y_copy(l, i):
        ty, tl = near[i]
        tq = ty * NL + tl
        return remote(yt.at[l, pl.ds(pl.multiple_of(tq * 64, 64), 64), :], yr.at[q, c], y_ss.at[l, i], y_rs.at[i, c],
                      dev(x, zh, ty, tl, l))

    def y_self(l):
        return pltpu.make_async_copy(yt.at[l, pl.ds(pl.multiple_of(q * 64, 64), 64), :], yr.at[q, l], y_rs.at[0, l])

    for l in range(2):
        part = fold(dot(split(gx[l]), qg[l]))
        yt[l] = part.T
        for i in range(1, 8):
            y_copy(l, i).start()

        @pl.when(c == l)
        def _():
            y_self(l).start()

        @pl.when(c != l)
        def _():
            y_copy(l, 0).start()

    def y_arrived(i, k):
        dy, dl = i // NL, i % NL
        sq = ((y + NY - dy) % NY) * NL + (zl + dl) % NL
        return remote(yr.at[sq, k], yr.at[sq, k], y_ss.at[0, i], y_rs.at[i, k], dev(x, zh, y, zl, 1 - c))

    for i in range(8):
        for k in range(NC):
            y_arrived(i, k).wait_recv()
    t4[...] = jnp.sum(yr[...], axis=0).reshape(128, 256)

    def t_copy(d):
        to = (zh + d) % NZ
        return remote(t4.at[pl.ds(pl.multiple_of(to * 32, 32), 32), :], mid.at[zh], t_ss.at[d], t_rs.at[d],
                      dev(x, to, y, zl, c))

    for d in range(1, NZ):
        t_copy(d).start()
    mid[zh] = t4[pl.ds(pl.multiple_of(zh * 32, 32), 32), :]

    spec_a = qa[0, 64:65, :].astype(F32)
    spot = (x * 2 + zh // 2) * 2 + q // 4
    line = qa[spot, 64:80, :][1:2, :256].astype(F32)
    start = (q % 4) * 64 + (zh % 2) * 32
    pick = lax.broadcasted_iota(jnp.int32, (32, 256), 1) == lax.broadcasted_iota(jnp.int32, (32, 256), 0) + start
    spec_g = jnp.sum(jnp.where(pick, line, 0.0), axis=1, keepdims=True)
    basis = qa[:, 0:64, :].reshape(1024, 1024)

    for d in range(1, NZ):
        t_copy(d).wait_recv()
    turned = jnp.concatenate([mid[k] for k in range(NZ)], axis=1)
    rotated = fold(dot(split(turned), basis))
    scaled = rotated / (spec_g * spec_a + DAMPING)
    wide = fold(dot(split(scaled), basis, ((1,), (1,))))
    for k in range(NZ):
        wt[k] = wide[:, k * 256:(k + 1) * 256]

    def w_copy(d):
        to = (zh + d) % NZ
        return remote(wt.at[to], wr.at[pl.ds(pl.multiple_of(zh * 32, 32), 32), :], w_ss.at[d], w_rs.at[d],
                      dev(x, to, y, zl, c))

    for d in range(1, NZ):
        w_copy(d).start()
    wr[pl.ds(pl.multiple_of(zh * 32, 32), 32), :] = wt[zh]
    for d in range(1, NZ):
        w_copy(d).wait_recv()

    def a_copy(k, i):
        ty, tl = near[i]
        return remote(wr.at[pl.ds(k * 64, 64), :], wall.at[c, pl.ds(pl.multiple_of(q * 64, 64), 64), :], a_ss.at[k, i],
                      a_rs.at[c, i], dev(x, zh, ty, tl, k))

    def a_self(k):
        return pltpu.make_async_copy(wr.at[pl.ds(k * 64, 64), :], wall.at[k, pl.ds(pl.multiple_of(q * 64, 64), 64), :],
                                     a_rs.at[k, 0])

    for i in range(1, 8):
        for k in range(NC):
            a_copy(k, i).start()
    for k in range(NC):
        @pl.when(c == k)
        def _():
            a_self(k).start()

        @pl.when(c != k)
        def _():
            a_copy(k, 0).start()

    def a_arrived(l, i):
        dy, dl = i // NL, i % NL
        sq = ((y + NY - dy) % NY) * NL + (zl + dl) % NL
        block = wall.at[l, pl.ds(pl.multiple_of(sq * 64, 64), 64), :]
        return remote(block, block, a_ss.at[0, i], a_rs.at[l, i], dev(x, zh, y, zl, 1 - c))

    def c_copy(l):
        return remote(mx.at[l, 1 - c], mc.at[l], c_ss.at[l], c_rs.at[l], dev(x, zh, y, zl, 1 - c))

    def o_copy(l, d):
        to = (x + d) % NX
        return remote(ms.at[l, pl.ds(pl.multiple_of(to * 64, 64), 64), :], orc.at[l, x], o_ss.at[l, d], o_rs.at[l, d],
                      dev(to, zh, y, zl, c))

    for l in range(2):
        for i in range(8):
            a_arrived(l, i).wait_recv()
        part = fold(dot(split(wall[l].T), qg[l], ((1,), (1,))))
        mx[l, 0] = part[:, :256]
        mx[l, 1] = part[:, 256:]
        c_copy(l).start()
    for l in range(2):
        c_copy(l).wait_recv()
        ms[l] = mx[l, c] + mc[l]
        for d in range(1, NX):
            o_copy(l, d).start()
        orc[l, x] = ms[l, pl.ds(pl.multiple_of(x * 64, 64), 64), :]
    for l in range(2):
        for d in range(1, NX):
            o_copy(l, d).wait_recv()
        out[l] = (orc[l, 0] + orc[l, 1]) + (orc[l, 2] + orc[l, 3])

    for l in range(2):
        for i in range(1, 8):
            y_copy(l, i).wait_send()

        @pl.when(c != l)
        def _():
            y_copy(l, 0).wait_send()
            a_copy(l, 0).wait_send()
        c_copy(l).wait_send()
        for d in range(1, NX):
            o_copy(l, d).wait_send()
        for i in range(1, 8):
            a_copy(l, i).wait_send()
    for d in range(1, NZ):
        t_copy(d).wait_send()
        w_copy(d).wait_send()


def turn(qg, qa, gx):
    dma = pltpu.SemaphoreType.DMA
    vmem = pl.BlockSpec(memory_space=pltpu.VMEM)
    return pl.pallas_call(
        turn_kernel,
        out_shape=jax.ShapeDtypeStruct((2, 64, 256), F32),
        in_specs=[vmem] * 3,
        out_specs=vmem,
        scratch_shapes=[
            pltpu.VMEM((2, 512, 256), F32),
            pltpu.VMEM((8, 2, 64, 256), F32),
            pltpu.VMEM((128, 256), F32),
            pltpu.VMEM((4, 32, 256), F32),
            pltpu.VMEM((4, 32, 256), F32),
            pltpu.VMEM((128, 256), F32),
            pltpu.VMEM((2, 512, 256), F32),
            pltpu.VMEM((2, 2, 256, 256), F32),
            pltpu.VMEM((2, 256, 256), F32),
            pltpu.VMEM((2, 256, 256), F32),
            pltpu.VMEM((2, 4, 64, 256), F32),
            dma((2, 8)), dma((8, 2)), dma((4,)), dma((4,)), dma((4,)), dma((4,)), dma((2, 8)), dma((2, 8)),
            dma((2,)), dma((2,)), dma((2, 4)), dma((2, 4)),
        ],
        compiler_params=pltpu.CompilerParams(collective_id=15, has_side_effects=True, vmem_limit_bytes=40 * 2**20),
        name="turn",
    )(qg, qa, gx)


def local(owners, store_a, store_g, vals_a, vals_g, grads):
    grp = lax.axis_index("grp")
    first = owners[0] == FIXED_OWNER
    other = jnp.where(first, owners[1], owners[0])
    tiles = jnp.where(first, grads, grads[::-1])
    block = (grp % 4) * 4 + grp // 4
    piece = jnp.concatenate(
        [
            lax.dynamic_slice_in_dim(store_a[0], block * 64, 64, 0),
            vals_a,
            jnp.pad(vals_g, ((0, 0), (0, 1024 - 256))),
            jnp.zeros((14, 1024), BF16),
        ],
        axis=0,
    )
    qg, qa, gx = lax.switch(
        other, [functools.partial(spread, k) for k in range(FIXED_OWNER)], store_g[0], piece, tiles
    )
    result = turn(qg, qa, gx)
    return jnp.where(first, result, result[::-1])


def solution(mesh):
    return jax.shard_map(
        local,
        mesh=mesh,
        in_specs=(
            P(),
            P("rep", None, None),
            P("rep", "grp", None),
            P("rep", None),
            P("rep", "grp"),
            P(None, "rep", "grp"),
        ),
        out_specs=P(None, "rep", "grp"),
        check_vma=False,
    )
```

```python
import functools

import jax
import jax.numpy as jnp
from jax import lax
from jax.experimental import pallas as pl
from jax.experimental.pallas import tpu as pltpu
from jax.sharding import PartitionSpec as P

DAMPING = 0.1
MESH = pl.DeviceIdType.MESH
NX, NZ, NY, NL, NC = 4, 4, 4, 2, 2
FIXED_OWNER = 15
CHUNKS = 4
WIDE = 1024 + 128
BF16, F32 = jnp.bfloat16, jnp.float32


def coords():
    rep, grp = lax.axis_index("rep"), lax.axis_index("grp")
    return rep // NZ, rep % NZ, grp // (NL * NC), (grp // NC) % NL, grp % NC


def dev(x, zh, y, zl, c):
    return (x * NZ + zh, y * (NL * NC) + zl * NC + c)


def split(value):
    high = value.astype(BF16)
    low = (value - high.astype(F32)).astype(BF16)
    return jnp.concatenate([high, low], axis=0)


def fold(value):
    half = value.shape[0] // 2
    return value[:half] + value[half:]


def dot(left, right, dims=((1,), (0,))):
    return lax.dot_general(left, right, (dims, ((), ())), preferred_element_type=F32)


def kernel(other, owners, store_a, sg, vals_a, vals_g, grads, out, piece, gt, gx, qg, qa, yt, yr, t4, mid, wt, wr, wall, mx, mc, ms,
           orc, qg_ss, qg_rs, fw_ss, qa_ss, qa_rs, qf_ss, ga_ss, ga_rs, gx_ss, gx_rs, gc_ss, gc_rs, loc, y_ss, y_rs, t_ss, t_rs,
           w_ss, w_rs, a_ss, a_rs, c_ss, c_rs, o_ss, o_rs):
    x, zh, y, zl, c = coords()
    q = y * NL + zl
    rows = 256 // CHUNKS
    sources = (FIXED_OWNER, other)
    near = [((y + dy) % NY, (zl + dl) % NL) for dy in range(NY) for dl in range(NL)]
    barrier = pltpu.get_barrier_semaphore()
    peers = [dev((x + d) % NX, zh, y, zl, k) for d in range(1, NX) for k in range(NC)]
    peers += [dev(x, zh, ty, tl, k) for ty, tl in near[1:] for k in range(NC)] + [dev(x, zh, y, zl, 1 - c)]
    peers += [dev(x, (zh + d) % NZ, y, zl, c) for d in range(1, NZ)]
    for peer in peers:
        pl.semaphore_signal(barrier, inc=1, device_id=peer, device_id_type=MESH)

    def remote(src, dst, ss, rs, to):
        return pltpu.make_async_remote_copy(src_ref=src, dst_ref=dst, send_sem=ss, recv_sem=rs, device_id=to,
                                            device_id_type=MESH)

    def mine(layer):
        return (x == sources[layer] // NZ) & (zh == sources[layer] % NZ)

    first = owners[0] == FIXED_OWNER
    gt[0] = jnp.where(first, grads[0], grads[1])
    gt[1] = jnp.where(first, grads[1], grads[0])

    grp = q * NC + c
    load = pltpu.make_async_copy(store_a.at[0, pl.ds(pl.multiple_of(((grp % 4) * 4 + grp // 4) * 64, 64), 64), :],
                                 piece.at[:, pl.ds(0, 1024)], loc.at[0])

    @pl.when(mine(0) | mine(1))
    def _():
        load.start()
        va, vg = vals_a[...].astype(F32), vals_g[...].astype(F32)
        lines = [va[:, i * 128:(i + 1) * 128] for i in range(8)] + [vg[:, i * 128:(i + 1) * 128] for i in range(2)]
        piece[:, 1024:WIDE] = jnp.concatenate(lines + [jnp.zeros((54, 128), F32)], axis=0).astype(BF16)
        load.wait()

    pl.semaphore_wait(barrier, len(peers))

    def qa_first(layer, d):
        tx = (sources[layer] // NZ + d) % NX
        return remote(piece.at[pl.ds(tx * 16, 16), :], qa.at[y, zl, c, tx], qa_ss.at[layer, d], qa_rs.at[c],
                      dev(tx, sources[layer] % NZ, y, zl, layer))

    def qa_local(layer):
        tx = sources[layer] // NZ
        return pltpu.make_async_copy(piece.at[pl.ds(tx * 16, 16), :], qa.at[y, zl, c, tx], qa_rs.at[c])

    def qg_first(layer, k, d, core):
        tx = (sources[layer] // NZ + d) % NX
        return remote(sg.at[0, pl.ds(k * rows, rows), pl.ds((tx * NC + core) * 512, 512)],
                      qg.at[layer, pl.ds(pl.multiple_of(c * 256 + k * rows, rows), rows), :],
                      qg_ss.at[layer, k, d, core], qg_rs.at[layer, c, k], dev(tx, sources[layer] % NZ, y, zl, core))

    def qg_local(layer, k, core):
        ox = sources[layer] // NZ
        return pltpu.make_async_copy(sg.at[0, pl.ds(k * rows, rows), pl.ds((ox * NC + core) * 512, 512)],
                                     qg.at[layer, pl.ds(core * 256 + k * rows, rows), :], qg_rs.at[layer, core, k])

    order = (2, 1, 3, 0)
    for layer in range(2):
        @pl.when(mine(layer))
        def _():
            for d in order:
                if d:
                    qa_first(layer, d).start()
                else:
                    @pl.when(c == layer)
                    def _():
                        qa_local(layer).start()

                    @pl.when(c != layer)
                    def _():
                        qa_first(layer, 0).start()

    tile = pl.ds(pl.multiple_of(x * 64, 64), 64), pl.ds(pl.multiple_of(c * 256, 256), 256)

    def g_x(l, d):
        return remote(gt.at[l], gx.at[l, tile[0], tile[1]], gx_ss.at[l, d - 1], gx_rs.at[l, d - 1],
                      dev((x + d) % NX, zh, y, zl, c))

    for l in range(2):
        for d in (2, 1, 3):
            g_x(l, d).start()
        gx[l, tile[0], tile[1]] = gt[l]

    for k in range(CHUNKS):
        for layer in range(2):
            @pl.when(mine(layer))
            def _():
                for d in order:
                    for core in range(NC):
                        if d:
                            qg_first(layer, k, d, core).start()
                        else:
                            @pl.when(c == core)
                            def _():
                                qg_local(layer, k, core).start()

                            @pl.when(c != core)
                            def _():
                                qg_first(layer, k, 0, core).start()

    def ring(layer, part):
        oz = sources[layer] % NZ
        if part == 0:
            return (zh + 1) % NZ, (zh + NZ - oz) % NZ
        return (zh + NZ - 1) % NZ, (oz + NZ - zh) % NZ

    def qa_on(layer, part):
        block = qa.at[y, zl, part, x]
        return remote(block, block, qf_ss.at[part], qa_rs.at[part], dev(x, ring(layer, part)[0], y, zl, layer))

    def qg_on(layer, part, k):
        block = qg.at[layer, pl.ds(pl.multiple_of(part * 256 + k * rows, rows), rows), :]
        return remote(block, block, fw_ss.at[layer, part, k], qg_rs.at[layer, part, k],
                      dev(x, ring(layer, part)[0], y, zl, c))

    def ring_step(t):
        for layer in range(2):
            for part in range(2):
                away = ring(layer, part)[1]
                if t < NZ:
                    @pl.when((away == t) & (c == layer))
                    def _():
                        qa_on(layer, part).wait_recv()
                        if t < NZ - 1:
                            qa_on(layer, part).start()
                k = t - 1 - away

                @pl.when((k >= 0) & (k < CHUNKS))
                def _():
                    qg_on(layer, part, k).wait_recv()

                    @pl.when(away < NZ - 1)
                    def _():
                        qg_on(layer, part, k).start()

    def over_x(block, stage):
        return [remote(block, block, ga_ss.at[stage, d - 1], ga_rs.at[stage, d - 1], dev((x + d) % NX, zh, y, zl, c))
                for d in (2, 1, 3)]

    def over_y(block, stage):
        return [remote(block, block, ga_ss.at[stage, d - 1], ga_rs.at[stage, d - 1], dev(x, zh, (y + d) % NY, zl, c))
                for d in (2, 1, 3)]

    def over_zl(block, stage):
        return [remote(block, block, ga_ss.at[stage, 0], ga_rs.at[stage, 0], dev(x, zh, y, 1 - zl, c))]

    stages = (
        (lambda: over_zl(qa.at[y, zl, :, x], 0), lambda: over_y(qa.at[y, :, :, x], 1), lambda: over_x(qa.at[:, :, :, x], 2)),
        (lambda: over_x(qa.at[y, zl, :, x], 0), lambda: over_zl(qa.at[y, zl], 1), lambda: over_y(qa.at[y], 2)),
    )

    def gather_start(stage):
        for core in range(NC):
            @pl.when(c == core)
            def _():
                if stage:
                    for copy in stages[core][stage - 1]():
                        copy.wait_recv()
                for copy in stages[core][stage]():
                    copy.start()

    def g_c(l):
        half = gx.at[l, :, tile[1]]
        return remote(half, half, gc_ss.at[l], gc_rs.at[l], dev(x, zh, y, zl, 1 - c))

    for t in range(CHUNKS + NZ):
        ring_step(t)
        if t == 3:
            gather_start(0)
            for l in range(2):
                for d in range(1, NX):
                    g_x(l, d).wait_recv()
                g_c(l).start()
        if t == 5:
            gather_start(1)
    gather_start(2)
    for l in range(2):
        g_c(l).wait_recv()

    def y_copy(l, i):
        ty, tl = near[i]
        tq = ty * NL + tl
        return remote(yt.at[l, pl.ds(pl.multiple_of(tq * 64, 64), 64), :], yr.at[q, c], y_ss.at[l, i], y_rs.at[i, c],
                      dev(x, zh, ty, tl, l))

    def y_self(l):
        return pltpu.make_async_copy(yt.at[l, pl.ds(pl.multiple_of(q * 64, 64), 64), :], yr.at[q, l], y_rs.at[0, l])

    for l in range(2):
        part = fold(dot(split(gx[l]), qg[l]))
        yt[l] = part.T
        for i in range(1, 8):
            y_copy(l, i).start()

        @pl.when(c == l)
        def _():
            y_self(l).start()

        @pl.when(c != l)
        def _():
            y_copy(l, 0).start()

    def y_arrived(i, k):
        dy, dl = i // NL, i % NL
        sq = ((y + NY - dy) % NY) * NL + (zl + dl) % NL
        return remote(yr.at[sq, k], yr.at[sq, k], y_ss.at[0, i], y_rs.at[i, k], dev(x, zh, y, zl, 1 - c))

    for i in range(8):
        for k in range(NC):
            y_arrived(i, k).wait_recv()
    t4[...] = jnp.sum(yr[...], axis=0).reshape(128, 256)

    def t_copy(d):
        to = (zh + d) % NZ
        return remote(t4.at[pl.ds(pl.multiple_of(to * 32, 32), 32), :], mid.at[zh], t_ss.at[d], t_rs.at[d],
                      dev(x, to, y, zl, c))

    for d in range(1, NZ):
        t_copy(d).start()
    mid[zh] = t4[pl.ds(pl.multiple_of(zh * 32, 32), 32), :]

    for d in range(1, NZ):
        t_copy(d).wait_recv()
    for core in range(NC):
        @pl.when(c == core)
        def _():
            for copy in stages[core][2]():
                copy.wait_recv()

    spec_a = jnp.concatenate([qa[0, 0, 0, 0, :, 1024:WIDE].astype(F32)[i:i + 1] for i in range(8)], axis=1)
    spot = (x * 2 + zh // 2) * 2 + q // 4
    line = qa[spot // 4, (spot // 2) % 2, spot % 2, 0, :, 1024:WIDE].astype(F32)
    line = jnp.concatenate([line[8:9], line[9:10]], axis=1)
    start = (q % 4) * 64 + (zh % 2) * 32
    pick = lax.broadcasted_iota(jnp.int32, (32, 256), 1) == lax.broadcasted_iota(jnp.int32, (32, 256), 0) + start
    spec_g = jnp.sum(jnp.where(pick, line, 0.0), axis=1, keepdims=True)
    basis = qa[:, :, :, :, :, 0:1024].reshape(1024, 1024)

    turned = jnp.concatenate([mid[k] for k in range(NZ)], axis=1)
    rotated = fold(dot(split(turned), basis))
    scaled = rotated / (spec_g * spec_a + DAMPING)
    wide = fold(dot(split(scaled), basis, ((1,), (1,))))
    for k in range(NZ):
        wt[k] = wide[:, k * 256:(k + 1) * 256]

    def w_copy(d):
        to = (zh + d) % NZ
        return remote(wt.at[to], wr.at[pl.ds(pl.multiple_of(zh * 32, 32), 32), :], w_ss.at[d], w_rs.at[d],
                      dev(x, to, y, zl, c))

    for d in range(1, NZ):
        w_copy(d).start()
    wr[pl.ds(pl.multiple_of(zh * 32, 32), 32), :] = wt[zh]
    for d in range(1, NZ):
        w_copy(d).wait_recv()

    def a_copy(k, i):
        ty, tl = near[i]
        return remote(wr.at[pl.ds(k * 64, 64), :], wall.at[c, pl.ds(pl.multiple_of(q * 64, 64), 64), :], a_ss.at[k, i],
                      a_rs.at[c, i], dev(x, zh, ty, tl, k))

    def a_self(k):
        return pltpu.make_async_copy(wr.at[pl.ds(k * 64, 64), :], wall.at[k, pl.ds(pl.multiple_of(q * 64, 64), 64), :],
                                     a_rs.at[k, 0])

    for i in range(1, 8):
        for k in range(NC):
            a_copy(k, i).start()
    for k in range(NC):
        @pl.when(c == k)
        def _():
            a_self(k).start()

        @pl.when(c != k)
        def _():
            a_copy(k, 0).start()

    def a_arrived(l, i):
        dy, dl = i // NL, i % NL
        sq = ((y + NY - dy) % NY) * NL + (zl + dl) % NL
        block = wall.at[l, pl.ds(pl.multiple_of(sq * 64, 64), 64), :]
        return remote(block, block, a_ss.at[0, i], a_rs.at[l, i], dev(x, zh, y, zl, 1 - c))

    def c_copy(l):
        return remote(mx.at[l, 1 - c], mc.at[l], c_ss.at[l], c_rs.at[l], dev(x, zh, y, zl, 1 - c))

    def o_copy(l, d):
        to = (x + d) % NX
        return remote(ms.at[l, pl.ds(pl.multiple_of(to * 64, 64), 64), :], orc.at[l, x], o_ss.at[l, d], o_rs.at[l, d],
                      dev(to, zh, y, zl, c))

    for l in range(2):
        for i in range(8):
            a_arrived(l, i).wait_recv()
        part = fold(dot(split(wall[l].T), qg[l], ((1,), (1,))))
        mx[l, 0] = part[:, :256]
        mx[l, 1] = part[:, 256:]
        c_copy(l).start()
    for l in range(2):
        c_copy(l).wait_recv()
        ms[l] = mx[l, c] + mc[l]
        for d in range(1, NX):
            o_copy(l, d).start()
        orc[l, x] = ms[l, pl.ds(pl.multiple_of(x * 64, 64), 64), :]
    for l in range(2):
        for d in range(1, NX):
            o_copy(l, d).wait_recv()
        out[l] = (orc[l, 0] + orc[l, 1]) + (orc[l, 2] + orc[l, 3])

    for l in range(2):
        for i in range(1, 8):
            y_copy(l, i).wait_send()

        @pl.when(c != l)
        def _():
            y_copy(l, 0).wait_send()
            a_copy(l, 0).wait_send()
        c_copy(l).wait_send()
        for d in range(1, NX):
            o_copy(l, d).wait_send()
        for i in range(1, 8):
            a_copy(l, i).wait_send()
    for d in range(1, NZ):
        t_copy(d).wait_send()
        w_copy(d).wait_send()

    for l in range(2):
        g_c(l).wait_send()
        for d in range(1, NX):
            g_x(l, d).wait_send()
    for core in range(NC):
        @pl.when(c == core)
        def _():
            for stage in range(3):
                for copy in stages[core][stage]():
                    copy.wait_send()
    for layer in range(2):
        for part in range(2):
            @pl.when(ring(layer, part)[1] < NZ - 1)
            def _():
                @pl.when(c == layer)
                def _():
                    qa_on(layer, part).wait_send()
                for k in range(CHUNKS):
                    qg_on(layer, part, k).wait_send()

        @pl.when(mine(layer))
        def _():
            for d in order:
                if d:
                    qa_first(layer, d).wait_send()
                else:
                    @pl.when(c != layer)
                    def _():
                        qa_first(layer, 0).wait_send()
            for k in range(CHUNKS):
                for d in order:
                    for core in range(NC):
                        if d:
                            qg_first(layer, k, d, core).wait_send()
                        else:
                            @pl.when(c != core)
                            def _():
                                qg_first(layer, k, 0, core).wait_send()


def run(other, owners, store_a, store_g, vals_a, vals_g, grads):
    dma = pltpu.SemaphoreType.DMA
    vmem, anywhere = pl.BlockSpec(memory_space=pltpu.VMEM), pl.BlockSpec(memory_space=pl.ANY)
    return pl.pallas_call(
        functools.partial(kernel, other),
        out_shape=jax.ShapeDtypeStruct((2, 64, 256), F32),
        in_specs=[pl.BlockSpec(memory_space=pltpu.SMEM), anywhere, anywhere, vmem, vmem, vmem],
        out_specs=vmem,
        scratch_shapes=[
            pltpu.VMEM((64, WIDE), BF16),
            pltpu.VMEM((2, 64, 256), F32),
            pltpu.VMEM((2, 256, 512), F32),
            pltpu.VMEM((2, 512, 512), BF16),
            pltpu.VMEM((NY, NL, NC, NX, 16, WIDE), BF16),
            pltpu.VMEM((2, 512, 256), F32),
            pltpu.VMEM((8, 2, 64, 256), F32),
            pltpu.VMEM((128, 256), F32),
            pltpu.VMEM((4, 32, 256), F32),
            pltpu.VMEM((4, 32, 256), F32),
            pltpu.VMEM((128, 256), F32),
            pltpu.VMEM((2, 512, 256), F32),
            pltpu.VMEM((2, 2, 256, 256), F32),
            pltpu.VMEM((2, 256, 256), F32),
            pltpu.VMEM((2, 256, 256), F32),
            pltpu.VMEM((2, 4, 64, 256), F32),
            dma((2, CHUNKS, NX, NC)), dma((2, NC, CHUNKS)), dma((2, 2, CHUNKS)),
            dma((2, NX)), dma((2,)), dma((2,)), dma((3, 3)), dma((3, 3)),
            dma((2, 3)), dma((2, 3)), dma((2,)), dma((2,)), dma((1,)),
            dma((2, 8)), dma((8, 2)), dma((4,)), dma((4,)), dma((4,)), dma((4,)), dma((2, 8)), dma((2, 8)),
            dma((2,)), dma((2,)), dma((2, 4)), dma((2, 4)),
        ],
        compiler_params=pltpu.CompilerParams(collective_id=other, has_side_effects=True, vmem_limit_bytes=40 * 2**20),
        name=f"kfac_{other}",
    )(owners, store_a, store_g, vals_a, vals_g, grads)


def local(owners, store_a, store_g, vals_a, vals_g, grads):
    first = owners[0] == FIXED_OWNER
    other = jnp.where(first, owners[1], owners[0])
    variants = [functools.partial(run, k) for k in range(FIXED_OWNER)]
    result = lax.switch(other, variants, owners, store_a, store_g, vals_a, vals_g, grads)
    return jnp.where(first, result, result[::-1])


def solution(mesh):
    return jax.shard_map(
        local,
        mesh=mesh,
        in_specs=(
            P(),
            P("rep", None, None),
            P("rep", "grp", None),
            P("rep", None),
            P("rep", "grp"),
            P(None, "rep", "grp"),
        ),
        out_specs=P(None, "rep", "grp"),
        check_vma=False,
    )
```

```python
import functools

import jax
import jax.numpy as jnp
from jax import lax
from jax.experimental import pallas as pl
from jax.experimental.pallas import tpu as pltpu
from jax.sharding import PartitionSpec as P

DAMPING = 0.1
MESH = pl.DeviceIdType.MESH
NX, NZ, NY, NL, NC = 4, 4, 4, 2, 2
NEAR = NY * NL
FIXED_OWNER = 15
CHUNKS = 8
SLACK = 2
FLIGHT = 2
LAG = 4
READY = CHUNKS + 3 * SLACK + 1
ROWS = 256 // CHUNKS
WIDE = 1024 + 128
BF16, F32, I16 = jnp.bfloat16, jnp.float32, jnp.int16


def coords():
    rep, grp = lax.axis_index("rep"), lax.axis_index("grp")
    return rep // NZ, rep % NZ, grp // (NL * NC), (grp // NC) % NL, grp % NC


def dev(x, zh, y, zl, c):
    return (x * NZ + zh, y * (NL * NC) + zl * NC + c)


def remote(src, dst, ss, rs, to):
    return pltpu.make_async_remote_copy(src_ref=src, dst_ref=dst, send_sem=ss, recv_sem=rs, device_id=to, device_id_type=MESH)


def at(start, size):
    return pl.ds(pl.multiple_of(start, size), size)


def split(value):
    high = value.astype(BF16)
    low = (value - high.astype(F32)).astype(BF16)
    return jnp.concatenate([high, low], axis=0)


def fold(value):
    half = value.shape[0] // 2
    return value[:half] + value[half:]


def code(value):
    top = jnp.maximum(jnp.max(jnp.abs(value), axis=0, keepdims=True), 1e-30)
    scale = top * (1 / 32767)
    digits = jnp.round(value * (32767 / top)).astype(jnp.int32).astype(jnp.int16)
    return digits, jnp.concatenate([scale[:, :128], scale[:, 128:], jnp.zeros((6, 128), F32)], axis=0)


def decode(digits, tile):
    scale = jnp.concatenate([tile[0:1], tile[1:2]], axis=1)
    return digits.astype(jnp.int32).astype(F32) * scale


def dot(left, right, dims=((1,), (0,))):
    return lax.dot_general(left, right, (dims, ((), ())), preferred_element_type=F32)


def kernel(other, owners, store_a, sg, vals_a, vals_g, grads, out, piece, gt, gx, qg, qa, yt, ys, yr, yv, t4, mid, wt, wr, wc, ws, wall, wv, wf, mx, mc, ms,
           orc, rot, qg_ss, qg_rs, fw_ss, qa_ss, qa_rs, qf_ss, ga_ss, ga_rs, gx_ss, gx_rs, gc_ss, gc_rs, loc, y_ss, y_rs, s_ss, s_rs, t_ss, t_rs,
           w_ss, w_rs, a_ss, a_rs, v_ss, v_rs, c_ss, c_rs, o_ss, o_rs):
    x, zh, y, zl, c = coords()
    q = y * NL + zl

    def near(i):
        return (y + i // NL) % NY, (zl + i % NL) % NL

    barrier = pltpu.get_barrier_semaphore()

    def greet(peer):
        pl.semaphore_signal(barrier, inc=1, device_id=peer, device_id_type=MESH)

    @pl.loop(1, NX)
    def _(d):
        greet(dev((x + d) % NX, zh, y, zl, 0))
        greet(dev((x + d) % NX, zh, y, zl, 1))
        greet(dev(x, (zh + d) % NZ, y, zl, c))

    @pl.loop(1, NEAR)
    def _(i):
        ty, tl = near(i)
        greet(dev(x, zh, ty, tl, 0))
        greet(dev(x, zh, ty, tl, 1))

    greet(dev(x, zh, y, zl, 1 - c))

    first = owners[0] == FIXED_OWNER
    gt[0] = jnp.where(first, grads[0], grads[1])
    gt[1] = jnp.where(first, grads[1], grads[0])

    def source(layer):
        return [layer * (other // NZ) + (1 - layer) * (FIXED_OWNER // NZ), layer * (other % NZ) + (1 - layer) * (FIXED_OWNER % NZ)]

    def mine(layer):
        return (x == source(layer)[0]) & (zh == source(layer)[1])

    owner = mine(0) | mine(1)
    owned = jnp.where(mine(1), 1, 0)

    grp = q * NC + c

    @pl.when(owner)
    def _():
        load = pltpu.make_async_copy(store_a.at[0, at(((grp % 4) * 4 + grp // 4) * 64, 64), :], piece.at[:, pl.ds(0, 1024)], loc.at[0])
        load.start()
        va, vg = vals_a[...].astype(F32), vals_g[...].astype(F32)
        lines = [va[:, i * 128:(i + 1) * 128] for i in range(8)] + [vg[:, i * 128:(i + 1) * 128] for i in range(2)]
        piece[:, 1024:WIDE] = jnp.concatenate(lines + [jnp.zeros((54, 128), F32)], axis=0).astype(BF16)
        load.wait()

    pl.semaphore_wait(barrier, 3 * (NX - 1) + 2 * (NEAR - 1) + 1)

    def qa_first(d):
        tx = (x + d) % NX
        return remote(piece.at[at(tx * 16, 16), :], qa.at[y, zl, c, tx], qa_ss.at[d], qa_rs.at[c], dev(tx, zh, y, zl, owned))

    def qg_first(k, d, core):
        tx = (x + d) % NX
        return remote(sg.at[0, at(k * ROWS, ROWS), at((tx * NC + core) * 512, 512)], qg.at[owned, at(c * 256 + k * ROWS, ROWS), :],
                      qg_ss.at[k, d, core], qg_rs.at[owned, c, k], dev(tx, zh, y, zl, core))

    def qg_sent(k):
        for d in (2, 1, 3):
            for core in range(NC):
                qg_first(k, d, core).wait_send()
        qg_first(k, 0, 1 - c).wait_send()

    def qg_local(k):
        return pltpu.make_async_copy(sg.at[0, at(k * ROWS, ROWS), at((x * NC + c) * 512, 512)],
                                     qg.at[owned, at(c * 256 + k * ROWS, ROWS), :], qg_rs.at[owned, c, k])

    tile = at(x * 64, 64), at(c * 256, 256)

    def g_x(l, d):
        return remote(gt.at[l], gx.at[l, tile[0], tile[1]], gx_ss.at[l, d], gx_rs.at[l, d], dev((x + d) % NX, zh, y, zl, c))

    def g_c(l):
        half = gx.at[l, :, tile[1]]
        return remote(half, half, gc_ss.at[l], gc_rs.at[l], dev(x, zh, y, zl, 1 - c))

    @pl.when(owner)
    def _():
        @pl.loop(1, NX)
        def _(d):
            qa_first(d).start()

        @pl.when(c == owned)
        def _():
            pltpu.make_async_copy(piece.at[at(x * 16, 16), :], qa.at[y, zl, c, x], qa_rs.at[c]).start()

        @pl.when(c != owned)
        def _():
            qa_first(0).start()

    def ring(layer, part):
        oz = source(layer)[1]
        return (zh + 1 + 2 * part) % NZ, (1 - part) * ((zh + NZ - oz) % NZ) + part * ((oz + NZ - zh) % NZ)

    def qa_on(part):
        block = qa.at[y, zl, part, x]
        return remote(block, block, qf_ss.at[part], qa_rs.at[part], dev(x, ring(c, part)[0], y, zl, c))

    def qg_on(layer, part, k):
        block = qg.at[layer, at(part * 256 + k * ROWS, ROWS), :]
        return remote(block, block, fw_ss.at[layer, part, k], qg_rs.at[layer, part, k], dev(x, ring(layer, part)[0], y, zl, c))

    def over_x(block, stage):
        return [remote(block, block, ga_ss.at[stage, d], ga_rs.at[stage, d], dev((x + d) % NX, zh, y, zl, c)) for d in (2, 1, 3)]

    def over_y(block, stage):
        return [remote(block, block, ga_ss.at[stage, d], ga_rs.at[stage, d], dev(x, zh, (y + d) % NY, zl, c)) for d in (2, 1, 3)]

    def over_zl(block, stage):
        return [remote(block, block, ga_ss.at[stage, 0], ga_rs.at[stage, 0], dev(x, zh, y, 1 - zl, c))]

    stages = (
        (lambda: over_zl(qa.at[y, zl, :, x], 0), lambda: over_y(qa.at[y, :, :, x], 1), lambda: over_x(qa.at[:, :, :, x], 2)),
        (lambda: over_x(qa.at[y, zl, :, x], 0), lambda: over_zl(qa.at[y, zl], 1), lambda: over_y(qa.at[y], 2)),
    )

    def per_core(act):
        for core in range(NC):
            @pl.when(c == core)
            def _():
                act(stages[core])

    def gather_start(stage):
        def act(mine):
            if stage:
                for copy in mine[stage - 1]():
                    copy.wait_recv()
            for copy in mine[stage]():
                copy.start()
        per_core(act)

    def y_copy(l, i):
        ty, tl = near(i)
        tq = ty * NL + tl
        return [remote(yt.at[l, tq], yr.at[q, c], y_ss.at[l, i], y_rs.at[i, c], dev(x, zh, ty, tl, l)),
                remote(ys.at[l, tq], yv.at[q, c], s_ss.at[l, i], s_rs.at[i, c], dev(x, zh, ty, tl, l))]

    @pl.loop(0, READY + LAG + 1)
    def _(t):
        @pl.when(owner & (t < CHUNKS))
        def _():
            @pl.when(t >= FLIGHT)
            def _():
                qg_sent(t - FLIGHT)
            for d in (2, 1, 3):
                for core in range(NC):
                    qg_first(t, d, core).start()
            qg_first(t, 0, 1 - c).start()
            qg_local(t).start()

        @pl.loop(0, 2)
        def _(part):
            away = ring(c, part)[1]

            @pl.when(away * SLACK == t)
            def _():
                qa_on(part).wait_recv()

                @pl.when(away < NZ - 1)
                def _():
                    qa_on(part).start()

        @pl.loop(0, 4)
        def _(flow):
            layer, part = flow // 2, flow % 2
            away = ring(layer, part)[1]
            k = t - 1 - SLACK * away - LAG * layer

            @pl.when((k >= 0) & (k < CHUNKS))
            def _():
                qg_on(layer, part, k).wait_recv()

                @pl.when(away < NZ - 1)
                def _():
                    @pl.when(k >= FLIGHT)
                    def _():
                        qg_on(layer, part, k - FLIGHT).wait_send()
                    qg_on(layer, part, k).start()

        @pl.when(t == 3)
        def _():
            @pl.loop(0, 2)
            def _(l):
                @pl.loop(1, NX)
                def _(d):
                    g_x(l, d).start()
                gx[l, tile[0], tile[1]] = gt[l]

        for stage, when in enumerate((7, 8, 9)):
            @pl.when(t == when)
            def _():
                gather_start(stage)

        @pl.when(t == READY - 3)
        def _():
            @pl.loop(0, 2)
            def _(l):
                @pl.loop(1, NX)
                def _(d):
                    g_x(l, d).wait_recv()
                g_c(l).start()

        @pl.when((t == READY) | (t == READY + LAG))
        def _():
            l = (t - READY) // LAG
            g_c(l).wait_recv()
            both = split(gx[l])

            @pl.loop(0, 4)
            def _(h):
                part = fold(dot(both, qg[l, :, at(h * 128, 128)])).T
                for k in range(2):
                    yt[l, h * 2 + k], ys[l, h * 2 + k] = code(part[k * 64:(k + 1) * 64])

            @pl.loop(1, NEAR)
            def _(i):
                for copy in y_copy(l, i):
                    copy.start()

            @pl.when(c == l)
            def _():
                yr[q, l] = yt[l, q]
                yv[q, l] = ys[l, q]

            @pl.when(c != l)
            def _():
                for copy in y_copy(l, 0):
                    copy.start()

    def y_wait(i, k):
        sq = ((y + NY - i // NL) % NY) * NL + (zl + i % NL) % NL
        remote(yr.at[sq, k], yr.at[sq, k], y_ss.at[0, i], y_rs.at[i, k], dev(x, zh, y, zl, 1 - c)).wait_recv()
        remote(yv.at[sq, k], yv.at[sq, k], s_ss.at[0, i], s_rs.at[i, k], dev(x, zh, y, zl, 1 - c)).wait_recv()

    y_wait(0, 1 - c)

    @pl.loop(1, NEAR)
    def _(i):
        for k in range(NC):
            y_wait(i, k)

    @pl.loop(0, NC)
    def _(k):
        t4[at(k * 64, 64), :] = lax.fori_loop(0, NEAR, lambda i, total: total + decode(yr[i, k], yv[i, k]), jnp.zeros((64, 256), F32))

    def t_copy(d):
        to = (zh + d) % NZ
        return remote(t4.at[at(to * 32, 32), :], mid.at[zh], t_ss.at[d], t_rs.at[d], dev(x, to, y, zl, c))

    for d in range(1, NZ):
        t_copy(d).start()
    mid[zh] = t4[at(zh * 32, 32), :]
    for d in range(1, NZ):
        t_copy(d).wait_recv()

    def act(mine):
        for copy in mine[2]():
            copy.wait_recv()
    per_core(act)

    spec_a = jnp.concatenate([qa[0, 0, 0, 0, :, 1024:WIDE].astype(F32)[i:i + 1] for i in range(8)], axis=1)
    spot = (x * 2 + zh // 2) * 2 + q // 4
    line = qa[spot // 4, (spot // 2) % 2, spot % 2, 0, :, 1024:WIDE].astype(F32)
    line = jnp.concatenate([line[8:9], line[9:10]], axis=1)
    start = (q % 4) * 64 + (zh % 2) * 32
    pick = lax.broadcasted_iota(jnp.int32, (32, 256), 1) == lax.broadcasted_iota(jnp.int32, (32, 256), 0) + start
    spec_g = jnp.sum(jnp.where(pick, line, 0.0), axis=1, keepdims=True)
    turned = split(jnp.concatenate([mid[k] for k in range(NZ)], axis=1))

    @pl.loop(0, 4)
    def _(k):
        rot[k] = fold(dot(turned, qa[:, :, :, :, :, at(k * 256, 256)].reshape(1024, 256)))

    rotated = jnp.concatenate([rot[k] for k in range(4)], axis=1)
    scaled = split(rotated / (spec_g * spec_a + DAMPING))

    @pl.loop(0, 4)
    def _(k):
        wt[k] = fold(dot(scaled, qa[k, :, :, :, :, 0:1024].reshape(256, 1024), ((1,), (1,))))

    def w_copy(d):
        to = (zh + d) % NZ
        return remote(wt.at[to], wr.at[at(zh * 32, 32), :], w_ss.at[d], w_rs.at[d], dev(x, to, y, zl, c))

    for d in range(1, NZ):
        w_copy(d).start()
    wr[at(zh * 32, 32), :] = wt[zh]
    for d in range(1, NZ):
        w_copy(d).wait_recv()

    def a_copy(k, i):
        ty, tl = near(i)
        return [remote(wc.at[k], wall.at[c, q], a_ss.at[k, i], a_rs.at[c, i], dev(x, zh, ty, tl, k)),
                remote(ws.at[k], wv.at[c, q], v_ss.at[k, i], v_rs.at[c, i], dev(x, zh, ty, tl, k))]

    for k in range(NC):
        wc[k], ws[k] = code(wr[k * 64:(k + 1) * 64, :])

    @pl.loop(1, NEAR)
    def _(i):
        for k in range(NC):
            for copy in a_copy(k, i):
                copy.start()
    for copy in a_copy(1 - c, 0):
        copy.start()
    wall[c, q] = wc[c]
    wv[c, q] = ws[c]

    def c_copy(l):
        return remote(mx.at[l, 1 - c], mc.at[l], c_ss.at[l], c_rs.at[l], dev(x, zh, y, zl, 1 - c))

    def o_copy(l, d):
        to = (x + d) % NX
        return remote(ms.at[l, at(to * 64, 64), :], orc.at[l, x], o_ss.at[l, d], o_rs.at[l, d], dev(to, zh, y, zl, c))

    def a_wait(l, i):
        sq = ((y + NY - i // NL) % NY) * NL + (zl + i % NL) % NL
        remote(wall.at[l, sq], wall.at[l, sq], a_ss.at[0, i], a_rs.at[l, i], dev(x, zh, y, zl, 1 - c)).wait_recv()
        remote(wv.at[l, sq], wv.at[l, sq], v_ss.at[0, i], v_rs.at[l, i], dev(x, zh, y, zl, 1 - c)).wait_recv()

    @pl.loop(0, 2)
    def _(l):
        @pl.when(c != l)
        def _():
            a_wait(l, 0)

        @pl.loop(1, NEAR)
        def _(i):
            a_wait(l, i)

        @pl.loop(0, NEAR)
        def _(i):
            wf[at(i * 64, 64), :] = decode(wall[l, i], wv[l, i])
        both = split(wf[...].T)

        @pl.loop(0, 2)
        def _(h):
            mx[l, h] = fold(dot(both, qg[l, at(h * 256, 256), :], ((1,), (1,))))
        c_copy(l).start()

    for l in range(2):
        c_copy(l).wait_recv()
        ms[l] = mx[l, c] + mc[l]

        @pl.loop(1, NX)
        def _(d):
            o_copy(l, d).start()
        orc[l, x] = ms[l, at(x * 64, 64), :]
    for l in range(2):
        @pl.loop(1, NX)
        def _(d):
            o_copy(l, d).wait_recv()
        out[l] = (orc[l, 0] + orc[l, 1]) + (orc[l, 2] + orc[l, 3])

    @pl.loop(0, 2)
    def _(l):
        @pl.loop(1, NEAR)
        def _(i):
            for copy in y_copy(l, i) + a_copy(l, i):
                copy.wait_send()
        c_copy(l).wait_send()
        g_c(l).wait_send()

        @pl.loop(1, NX)
        def _(d):
            o_copy(l, d).wait_send()
            g_x(l, d).wait_send()
    for copy in y_copy(1 - c, 0) + a_copy(1 - c, 0):
        copy.wait_send()
    for d in range(1, NZ):
        t_copy(d).wait_send()
        w_copy(d).wait_send()

    def act(mine):
        for stage in range(3):
            for copy in mine[stage]():
                copy.wait_send()
    per_core(act)

    @pl.loop(0, 2)
    def _(part):
        @pl.when(ring(c, part)[1] < NZ - 1)
        def _():
            qa_on(part).wait_send()

    @pl.loop(0, 4)
    def _(flow):
        layer, part = flow // 2, flow % 2

        @pl.when(ring(layer, part)[1] < NZ - 1)
        def _():
            @pl.loop(CHUNKS - FLIGHT, CHUNKS)
            def _(k):
                qg_on(layer, part, k).wait_send()

    @pl.when(owner)
    def _():
        @pl.loop(1, NX)
        def _(d):
            qa_first(d).wait_send()

        @pl.when(c != owned)
        def _():
            qa_first(0).wait_send()

        for k in range(CHUNKS - FLIGHT, CHUNKS):
            qg_sent(k)


def run(other, owners, store_a, store_g, vals_a, vals_g, grads):
    dma = pltpu.SemaphoreType.DMA
    vmem, anywhere = pl.BlockSpec(memory_space=pltpu.VMEM), pl.BlockSpec(memory_space=pl.ANY)
    return pl.pallas_call(
        functools.partial(kernel, other),
        out_shape=jax.ShapeDtypeStruct((2, 64, 256), F32),
        in_specs=[pl.BlockSpec(memory_space=pltpu.SMEM), anywhere, anywhere, vmem, vmem, vmem],
        out_specs=vmem,
        scratch_shapes=[
            pltpu.VMEM((64, WIDE), BF16),
            pltpu.VMEM((2, 64, 256), F32),
            pltpu.VMEM((2, 256, 512), F32),
            pltpu.VMEM((2, 512, 512), BF16),
            pltpu.VMEM((NY, NL, NC, NX, 16, WIDE), BF16),
            pltpu.VMEM((2, NEAR, 64, 256), I16),
            pltpu.VMEM((2, NEAR, 8, 128), F32),
            pltpu.VMEM((NEAR, 2, 64, 256), I16),
            pltpu.VMEM((NEAR, 2, 8, 128), F32),
            pltpu.VMEM((128, 256), F32),
            pltpu.VMEM((4, 32, 256), F32),
            pltpu.VMEM((4, 32, 256), F32),
            pltpu.VMEM((128, 256), F32),
            pltpu.VMEM((2, 64, 256), I16),
            pltpu.VMEM((2, 8, 128), F32),
            pltpu.VMEM((2, NEAR, 64, 256), I16),
            pltpu.VMEM((2, NEAR, 8, 128), F32),
            pltpu.VMEM((512, 256), F32),
            pltpu.VMEM((2, 2, 256, 256), F32),
            pltpu.VMEM((2, 256, 256), F32),
            pltpu.VMEM((2, 256, 256), F32),
            pltpu.VMEM((2, 4, 64, 256), F32),
            pltpu.VMEM((4, 32, 256), F32),
            dma((CHUNKS, NX, NC)), dma((2, NC, CHUNKS)), dma((2, 2, CHUNKS)),
            dma((NX,)), dma((2,)), dma((2,)), dma((3, 4)), dma((3, 4)),
            dma((2, 4)), dma((2, 4)), dma((2,)), dma((2,)), dma((1,)),
            dma((2, 8)), dma((8, 2)), dma((2, 8)), dma((8, 2)), dma((4,)), dma((4,)), dma((4,)), dma((4,)),
            dma((2, 8)), dma((2, 8)), dma((2, 8)), dma((2, 8)),
            dma((2,)), dma((2,)), dma((2, 4)), dma((2, 4)),
        ],
        compiler_params=pltpu.CompilerParams(collective_id=other, has_side_effects=True, vmem_limit_bytes=40 * 2**20),
        name=f"kfac_{other}",
    )(owners, store_a, store_g, vals_a, vals_g, grads)


def local(owners, store_a, store_g, vals_a, vals_g, grads):
    first = owners[0] == FIXED_OWNER
    other = jnp.where(first, owners[1], owners[0])
    variants = [functools.partial(run, k) for k in range(FIXED_OWNER)]
    result = lax.switch(other, variants, owners, store_a, store_g, vals_a, vals_g, grads)
    return jnp.where(first, result, result[::-1])


def solution(mesh):
    return jax.shard_map(
        local,
        mesh=mesh,
        in_specs=(
            P(),
            P("rep", None, None),
            P("rep", "grp", None),
            P("rep", None),
            P("rep", "grp"),
            P(None, "rep", "grp"),
        ),
        out_specs=P(None, "rep", "grp"),
        check_vma=False,
    )
```

```python
import functools

import jax
import jax.numpy as jnp
from jax import lax
from jax.experimental import pallas as pl
from jax.experimental.pallas import tpu as pltpu
from jax.sharding import PartitionSpec as P

DAMPING = 0.1
MESH = pl.DeviceIdType.MESH
NX, NZ, NY, NL, NC = 4, 4, 4, 2, 2
NEAR = NY * NL
FIXED_OWNER = 15
CHUNKS = 8
SLACK = 2
FLIGHT = 4
LAG = 1
READY = CHUNKS + 3 * SLACK + 1
ROWS = 256 // CHUNKS
WIDE = 1024 + 128
BF16, F32, I16 = jnp.bfloat16, jnp.float32, jnp.int16


def coords():
    rep, grp = lax.axis_index("rep"), lax.axis_index("grp")
    return rep // NZ, rep % NZ, grp // (NL * NC), (grp // NC) % NL, grp % NC


def dev(x, zh, y, zl, c):
    return (x * NZ + zh, y * (NL * NC) + zl * NC + c)


def remote(src, dst, ss, rs, to):
    return pltpu.make_async_remote_copy(src_ref=src, dst_ref=dst, send_sem=ss, recv_sem=rs, device_id=to, device_id_type=MESH)


def at(start, size):
    return pl.ds(pl.multiple_of(start, size), size)


def split(value):
    high = value.astype(BF16)
    low = (value - high.astype(F32)).astype(BF16)
    return jnp.concatenate([high, low], axis=0)


def fold(value):
    half = value.shape[0] // 2
    return value[:half] + value[half:]


def code(value):
    top = jnp.maximum(jnp.max(jnp.abs(value), axis=0, keepdims=True), 1e-30)
    scale = top * (1 / 32767)
    digits = jnp.round(value * (32767 / top)).astype(jnp.int32).astype(jnp.int16)
    return digits, jnp.concatenate([scale[:, :128], scale[:, 128:], jnp.zeros((6, 128), F32)], axis=0)


def decode(digits, tile):
    scale = jnp.concatenate([tile[0:1], tile[1:2]], axis=1)
    return digits.astype(jnp.int32).astype(F32) * scale


def dot(left, right, dims=((1,), (0,))):
    return lax.dot_general(left, right, (dims, ((), ())), preferred_element_type=F32)


def kernel(other, owners, store_a, sg, vals_a, vals_g, grads, out, piece, gt, gx, qg, qa, yt, ys, yr, yv, t4, mid, wt, wr, wc, ws, wall, wv, wf, mx, mc, ms, mv,
           orc, orv, rot, qg_ss, qg_rs, fw_ss, qa_ss, qa_rs, qf_ss, ga_ss, ga_rs, gx_ss, gx_rs, gc_ss, gc_rs, loc, y_ss, y_rs, s_ss, s_rs, t_ss, t_rs,
           w_ss, w_rs, a_ss, a_rs, v_ss, v_rs, c_ss, c_rs, o_ss, o_rs, p_ss, p_rs):
    x, zh, y, zl, c = coords()
    q = y * NL + zl

    def near(i):
        return (y + i // NL) % NY, (zl + i % NL) % NL

    barrier = pltpu.get_barrier_semaphore()

    def greet(peer):
        pl.semaphore_signal(barrier, inc=1, device_id=peer, device_id_type=MESH)

    @pl.loop(1, NX)
    def _(d):
        greet(dev((x + d) % NX, zh, y, zl, 0))
        greet(dev((x + d) % NX, zh, y, zl, 1))
        greet(dev(x, (zh + d) % NZ, y, zl, c))

    @pl.loop(1, NEAR)
    def _(i):
        ty, tl = near(i)
        greet(dev(x, zh, ty, tl, 0))
        greet(dev(x, zh, ty, tl, 1))

    greet(dev(x, zh, y, zl, 1 - c))

    first = owners[0] == FIXED_OWNER
    gt[0] = jnp.where(first, grads[0], grads[1])
    gt[1] = jnp.where(first, grads[1], grads[0])

    def source(layer):
        return [layer * (other // NZ) + (1 - layer) * (FIXED_OWNER // NZ), layer * (other % NZ) + (1 - layer) * (FIXED_OWNER % NZ)]

    def mine(layer):
        return (x == source(layer)[0]) & (zh == source(layer)[1])

    owner = mine(0) | mine(1)
    owned = jnp.where(mine(1), 1, 0)

    grp = q * NC + c

    @pl.when(owner)
    def _():
        load = pltpu.make_async_copy(store_a.at[0, at(((grp % 4) * 4 + grp // 4) * 64, 64), :], piece.at[:, pl.ds(0, 1024)], loc.at[0])
        load.start()
        va, vg = vals_a[...].astype(F32), vals_g[...].astype(F32)
        lines = [va[:, i * 128:(i + 1) * 128] for i in range(8)] + [vg[:, i * 128:(i + 1) * 128] for i in range(2)]
        piece[:, 1024:WIDE] = jnp.concatenate(lines + [jnp.zeros((54, 128), F32)], axis=0).astype(BF16)
        load.wait()

    pl.semaphore_wait(barrier, 3 * (NX - 1) + 2 * (NEAR - 1) + 1)

    def qa_first(d):
        tx = (x + d) % NX
        return remote(piece.at[at(tx * 16, 16), :], qa.at[y, zl, c, tx], qa_ss.at[d], qa_rs.at[c], dev(tx, zh, y, zl, owned))

    def qg_first(k, d, core):
        tx = (x + d) % NX
        return remote(sg.at[0, at(k * ROWS, ROWS), at((tx * NC + core) * 512, 512)], qg.at[owned, at(c * 256 + k * ROWS, ROWS), :],
                      qg_ss.at[k, d, core], qg_rs.at[owned, c, k], dev(tx, zh, y, zl, core))

    def qg_sent(k):
        @pl.loop(0, (NX - 1) * NC)
        def _(i):
            qg_first(k, i // NC + 1, i % NC).wait_send()
        qg_first(k, 0, 1 - c).wait_send()

    def qg_local(k):
        return pltpu.make_async_copy(sg.at[0, at(k * ROWS, ROWS), at((x * NC + c) * 512, 512)],
                                     qg.at[owned, at(c * 256 + k * ROWS, ROWS), :], qg_rs.at[owned, c, k])

    tile = at(x * 64, 64), at(c * 256, 256)

    def g_x(l, d):
        return remote(gt.at[l], gx.at[l, tile[0], tile[1]], gx_ss.at[l, d], gx_rs.at[l, d], dev((x + d) % NX, zh, y, zl, c))

    def g_c(l):
        half = gx.at[l, :, tile[1]]
        return remote(half, half, gc_ss.at[l], gc_rs.at[l], dev(x, zh, y, zl, 1 - c))

    @pl.when(owner)
    def _():
        @pl.loop(1, NX)
        def _(d):
            qa_first(d).start()

        @pl.when(c == owned)
        def _():
            pltpu.make_async_copy(piece.at[at(x * 16, 16), :], qa.at[y, zl, c, x], qa_rs.at[c]).start()

        @pl.when(c != owned)
        def _():
            qa_first(0).start()

    def ring(layer, part):
        oz = source(layer)[1]
        return (zh + 1 + 2 * part) % NZ, (1 - part) * ((zh + NZ - oz) % NZ) + part * ((oz + NZ - zh) % NZ)

    def qa_on(part):
        block = qa.at[y, zl, part, x]
        return remote(block, block, qf_ss.at[part], qa_rs.at[part], dev(x, ring(c, part)[0], y, zl, c))

    def qg_on(layer, part, k):
        block = qg.at[layer, at(part * 256 + k * ROWS, ROWS), :]
        return remote(block, block, fw_ss.at[layer, part, k], qg_rs.at[layer, part, k], dev(x, ring(layer, part)[0], y, zl, c))

    def over_x(block, stage, act):
        @pl.loop(1, NX)
        def _(d):
            act(remote(block, block, ga_ss.at[stage, d], ga_rs.at[stage, d], dev((x + d) % NX, zh, y, zl, c)))

    def over_y(block, stage, act):
        @pl.loop(1, NY)
        def _(d):
            act(remote(block, block, ga_ss.at[stage, d], ga_rs.at[stage, d], dev(x, zh, (y + d) % NY, zl, c)))

    def over_zl(block, stage, act):
        act(remote(block, block, ga_ss.at[stage, 0], ga_rs.at[stage, 0], dev(x, zh, y, 1 - zl, c)))

    stages = (
        (lambda act: over_zl(qa.at[y, zl, :, x], 0, act), lambda act: over_y(qa.at[y, :, :, x], 1, act),
         lambda act: over_x(qa.at[:, :, :, x], 2, act)),
        (lambda act: over_x(qa.at[y, zl, :, x], 0, act), lambda act: over_zl(qa.at[y, zl], 1, act),
         lambda act: over_y(qa.at[y], 2, act)),
    )

    def gather(stage, act):
        for core in range(NC):
            @pl.when(c == core)
            def _():
                stages[core][stage](act)

    def begin(copy):
        copy.start()

    def arrived(copy):
        copy.wait_recv()

    def left(copy):
        copy.wait_send()

    def y_copy(l, i):
        ty, tl = near(i)
        tq = ty * NL + tl
        return [remote(yt.at[l, tq], yr.at[q, c], y_ss.at[l, i], y_rs.at[i, c], dev(x, zh, ty, tl, l)),
                remote(ys.at[l, tq], yv.at[q, c], s_ss.at[l, i], s_rs.at[i, c], dev(x, zh, ty, tl, l))]

    @pl.loop(0, READY + LAG + 1)
    def _(t):
        @pl.when(owner & (t < CHUNKS))
        def _():
            @pl.when(t >= FLIGHT)
            def _():
                qg_sent(t - FLIGHT)

            @pl.loop(0, (NX - 1) * NC)
            def _(i):
                qg_first(t, i // NC + 1, i % NC).start()
            qg_first(t, 0, 1 - c).start()
            qg_local(t).start()

        @pl.loop(0, 2)
        def _(part):
            away = ring(c, part)[1]

            @pl.when(away * SLACK == t)
            def _():
                qa_on(part).wait_recv()

                @pl.when(away < NZ - 1)
                def _():
                    qa_on(part).start()

        @pl.loop(0, 4)
        def _(flow):
            layer, part = flow // 2, flow % 2
            away = ring(layer, part)[1]
            k = t - 1 - SLACK * away - LAG * layer

            @pl.when((k >= 0) & (k < CHUNKS))
            def _():
                qg_on(layer, part, k).wait_recv()

                @pl.when(away < NZ - 1)
                def _():
                    @pl.when(k >= FLIGHT)
                    def _():
                        qg_on(layer, part, k - FLIGHT).wait_send()
                    qg_on(layer, part, k).start()

        @pl.when(t == 8)
        def _():
            @pl.loop(0, 2)
            def _(l):
                @pl.loop(1, NX)
                def _(d):
                    g_x(l, d).start()
                gx[l, tile[0], tile[1]] = gt[l]

        for stage, when in enumerate((7, 8, 9)):
            @pl.when(t == when)
            def _():
                if stage:
                    gather(stage - 1, arrived)
                gather(stage, begin)

        @pl.when(t == READY - 1)
        def _():
            @pl.loop(0, 2)
            def _(l):
                @pl.loop(1, NX)
                def _(d):
                    g_x(l, d).wait_recv()
                g_c(l).start()

        @pl.when((t == READY) | (t == READY + LAG))
        def _():
            l = (t - READY) // LAG
            g_c(l).wait_recv()
            both = split(gx[l])

            @pl.loop(0, 4)
            def _(h):
                part = fold(dot(both, qg[l, :, at(h * 128, 128)])).T
                for k in range(2):
                    yt[l, h * 2 + k], ys[l, h * 2 + k] = code(part[k * 64:(k + 1) * 64])

            @pl.loop(1, NEAR)
            def _(i):
                for copy in y_copy(l, i):
                    copy.start()

            @pl.when(c == l)
            def _():
                yr[q, l] = yt[l, q]
                yv[q, l] = ys[l, q]

            @pl.when(c != l)
            def _():
                for copy in y_copy(l, 0):
                    copy.start()

    def y_wait(i, k):
        sq = ((y + NY - i // NL) % NY) * NL + (zl + i % NL) % NL
        remote(yr.at[sq, k], yr.at[sq, k], y_ss.at[0, i], y_rs.at[i, k], dev(x, zh, y, zl, 1 - c)).wait_recv()
        remote(yv.at[sq, k], yv.at[sq, k], s_ss.at[0, i], s_rs.at[i, k], dev(x, zh, y, zl, 1 - c)).wait_recv()

    y_wait(0, 1 - c)

    @pl.loop(1, NEAR)
    def _(i):
        for k in range(NC):
            y_wait(i, k)

    @pl.loop(0, NC)
    def _(k):
        t4[at(k * 64, 64), :] = lax.fori_loop(0, NEAR, lambda i, total: total + decode(yr[i, k], yv[i, k]), jnp.zeros((64, 256), F32))

    def t_copy(d):
        to = (zh + d) % NZ
        return remote(t4.at[at(to * 32, 32), :], mid.at[zh], t_ss.at[d], t_rs.at[d], dev(x, to, y, zl, c))

    @pl.loop(1, NZ)
    def _(d):
        t_copy(d).start()

    mid[zh] = t4[at(zh * 32, 32), :]

    @pl.loop(1, NZ)
    def _(d):
        t_copy(d).wait_recv()

    gather(2, arrived)

    spec_a = jnp.concatenate([qa[0, 0, 0, 0, :, 1024:WIDE].astype(F32)[i:i + 1] for i in range(8)], axis=1)
    spot = (x * 2 + zh // 2) * 2 + q // 4
    line = qa[spot // 4, (spot // 2) % 2, spot % 2, 0, :, 1024:WIDE].astype(F32)
    line = jnp.concatenate([line[8:9], line[9:10]], axis=1)
    start = (q % 4) * 64 + (zh % 2) * 32
    pick = lax.broadcasted_iota(jnp.int32, (32, 256), 1) == lax.broadcasted_iota(jnp.int32, (32, 256), 0) + start
    spec_g = jnp.sum(jnp.where(pick, line, 0.0), axis=1, keepdims=True)
    turned = split(jnp.concatenate([mid[k] for k in range(NZ)], axis=1))

    @pl.loop(0, 4)
    def _(k):
        rot[k] = fold(dot(turned, qa[:, :, :, :, :, at(k * 256, 256)].reshape(1024, 256)))

    rotated = jnp.concatenate([rot[k] for k in range(4)], axis=1)
    scaled = split(rotated / (spec_g * spec_a + DAMPING))

    @pl.loop(0, 4)
    def _(k):
        wt[k] = fold(dot(scaled, qa[k, :, :, :, :, 0:1024].reshape(256, 1024), ((1,), (1,))))

    def w_copy(d):
        to = (zh + d) % NZ
        return remote(wt.at[to], wr.at[at(zh * 32, 32), :], w_ss.at[d], w_rs.at[d], dev(x, to, y, zl, c))

    @pl.loop(1, NZ)
    def _(d):
        w_copy(d).start()

    wr[at(zh * 32, 32), :] = wt[zh]

    @pl.loop(1, NZ)
    def _(d):
        w_copy(d).wait_recv()

    def a_copy(k, i):
        ty, tl = near(i)
        return [remote(wc.at[k], wall.at[c, q], a_ss.at[k, i], a_rs.at[c, i], dev(x, zh, ty, tl, k)),
                remote(ws.at[k], wv.at[c, q], v_ss.at[k, i], v_rs.at[c, i], dev(x, zh, ty, tl, k))]

    for k in range(NC):
        wc[k], ws[k] = code(wr[k * 64:(k + 1) * 64, :])

    @pl.loop(1, NEAR)
    def _(i):
        for k in range(NC):
            for copy in a_copy(k, i):
                copy.start()
    for copy in a_copy(1 - c, 0):
        copy.start()
    wall[c, q] = wc[c]
    wv[c, q] = ws[c]

    def c_copy(l):
        return remote(mx.at[l, 1 - c], mc.at[l], c_ss.at[l], c_rs.at[l], dev(x, zh, y, zl, 1 - c))

    def o_copy(l, d):
        to = (x + d) % NX
        return [remote(ms.at[l, to], orc.at[l, x], o_ss.at[l, d], o_rs.at[l, d], dev(to, zh, y, zl, c)),
                remote(mv.at[l, to], orv.at[l, x], p_ss.at[l, d], p_rs.at[l, d], dev(to, zh, y, zl, c))]

    def a_wait(l, i):
        sq = ((y + NY - i // NL) % NY) * NL + (zl + i % NL) % NL
        remote(wall.at[l, sq], wall.at[l, sq], a_ss.at[0, i], a_rs.at[l, i], dev(x, zh, y, zl, 1 - c)).wait_recv()
        remote(wv.at[l, sq], wv.at[l, sq], v_ss.at[0, i], v_rs.at[l, i], dev(x, zh, y, zl, 1 - c)).wait_recv()

    @pl.loop(0, 2)
    def _(l):
        @pl.when(c != l)
        def _():
            a_wait(l, 0)

        @pl.loop(1, NEAR)
        def _(i):
            a_wait(l, i)

        @pl.loop(0, NEAR)
        def _(i):
            wf[at(i * 64, 64), :] = decode(wall[l, i], wv[l, i])
        both = split(wf[...].T)

        @pl.loop(0, 2)
        def _(h):
            mx[l, h] = fold(dot(both, qg[l, at(h * 256, 256), :], ((1,), (1,))))
        c_copy(l).start()

    @pl.loop(0, 2)
    def _(l):
        c_copy(l).wait_recv()

        @pl.loop(0, NX)
        def _(k):
            ms[l, k], mv[l, k] = code(mx[l, c, at(k * 64, 64), :] + mc[l, at(k * 64, 64), :])

        @pl.loop(1, NX)
        def _(d):
            for copy in o_copy(l, d):
                copy.start()
        orc[l, x] = ms[l, x]
        orv[l, x] = mv[l, x]

    @pl.loop(0, 2)
    def _(l):
        @pl.loop(1, NX)
        def _(d):
            for copy in o_copy(l, d):
                copy.wait_recv()
        out[l] = lax.fori_loop(0, NX, lambda i, total: total + decode(orc[l, i], orv[l, i]), jnp.zeros((64, 256), F32))

    @pl.loop(0, 2)
    def _(l):
        @pl.loop(1, NEAR)
        def _(i):
            for copy in y_copy(l, i) + a_copy(l, i):
                copy.wait_send()
        c_copy(l).wait_send()
        g_c(l).wait_send()

        @pl.loop(1, NX)
        def _(d):
            for copy in o_copy(l, d):
                copy.wait_send()
            g_x(l, d).wait_send()
    for copy in y_copy(1 - c, 0) + a_copy(1 - c, 0):
        copy.wait_send()

    @pl.loop(1, NZ)
    def _(d):
        t_copy(d).wait_send()
        w_copy(d).wait_send()

    for stage in range(3):
        gather(stage, left)

    @pl.loop(0, 2)
    def _(part):
        @pl.when(ring(c, part)[1] < NZ - 1)
        def _():
            qa_on(part).wait_send()

    @pl.loop(0, 4)
    def _(flow):
        layer, part = flow // 2, flow % 2

        @pl.when(ring(layer, part)[1] < NZ - 1)
        def _():
            @pl.loop(CHUNKS - FLIGHT, CHUNKS)
            def _(k):
                qg_on(layer, part, k).wait_send()

    @pl.when(owner)
    def _():
        @pl.loop(1, NX)
        def _(d):
            qa_first(d).wait_send()

        @pl.when(c != owned)
        def _():
            qa_first(0).wait_send()

        @pl.loop(CHUNKS - FLIGHT, CHUNKS)
        def _(k):
            qg_sent(k)


def run(other, owners, store_a, store_g, vals_a, vals_g, grads):
    dma = pltpu.SemaphoreType.DMA
    vmem, anywhere = pl.BlockSpec(memory_space=pltpu.VMEM), pl.BlockSpec(memory_space=pl.ANY)
    return pl.pallas_call(
        functools.partial(kernel, other),
        out_shape=jax.ShapeDtypeStruct((2, 64, 256), F32),
        in_specs=[pl.BlockSpec(memory_space=pltpu.SMEM), anywhere, anywhere, vmem, vmem, vmem],
        out_specs=vmem,
        scratch_shapes=[
            pltpu.VMEM((64, WIDE), BF16),
            pltpu.VMEM((2, 64, 256), F32),
            pltpu.VMEM((2, 256, 512), F32),
            pltpu.VMEM((2, 512, 512), BF16),
            pltpu.VMEM((NY, NL, NC, NX, 16, WIDE), BF16),
            pltpu.VMEM((2, NEAR, 64, 256), I16),
            pltpu.VMEM((2, NEAR, 8, 128), F32),
            pltpu.VMEM((NEAR, 2, 64, 256), I16),
            pltpu.VMEM((NEAR, 2, 8, 128), F32),
            pltpu.VMEM((128, 256), F32),
            pltpu.VMEM((4, 32, 256), F32),
            pltpu.VMEM((4, 32, 256), F32),
            pltpu.VMEM((128, 256), F32),
            pltpu.VMEM((2, 64, 256), I16),
            pltpu.VMEM((2, 8, 128), F32),
            pltpu.VMEM((2, NEAR, 64, 256), I16),
            pltpu.VMEM((2, NEAR, 8, 128), F32),
            pltpu.VMEM((512, 256), F32),
            pltpu.VMEM((2, 2, 256, 256), F32),
            pltpu.VMEM((2, 256, 256), F32),
            pltpu.VMEM((2, 4, 64, 256), I16),
            pltpu.VMEM((2, 4, 8, 128), F32),
            pltpu.VMEM((2, 4, 64, 256), I16),
            pltpu.VMEM((2, 4, 8, 128), F32),
            pltpu.VMEM((4, 32, 256), F32),
            dma((CHUNKS, NX, NC)), dma((2, NC, CHUNKS)), dma((2, 2, CHUNKS)),
            dma((NX,)), dma((2,)), dma((2,)), dma((3, 4)), dma((3, 4)),
            dma((2, 4)), dma((2, 4)), dma((2,)), dma((2,)), dma((1,)),
            dma((2, 8)), dma((8, 2)), dma((2, 8)), dma((8, 2)), dma((4,)), dma((4,)), dma((4,)), dma((4,)),
            dma((2, 8)), dma((2, 8)), dma((2, 8)), dma((2, 8)),
            dma((2,)), dma((2,)), dma((2, 4)), dma((2, 4)), dma((2, 4)), dma((2, 4)),
        ],
        compiler_params=pltpu.CompilerParams(collective_id=other, has_side_effects=True, vmem_limit_bytes=40 * 2**20),
        name=f"kfac_{other}",
    )(owners, store_a, store_g, vals_a, vals_g, grads)


def local(owners, store_a, store_g, vals_a, vals_g, grads):
    first = owners[0] == FIXED_OWNER
    other = jnp.where(first, owners[1], owners[0])
    variants = [functools.partial(run, k) for k in range(FIXED_OWNER)]
    result = lax.switch(other, variants, owners, store_a, store_g, vals_a, vals_g, grads)
    return jnp.where(first, result, result[::-1])


def solution(mesh):
    return jax.shard_map(
        local,
        mesh=mesh,
        in_specs=(
            P(),
            P("rep", None, None),
            P("rep", "grp", None),
            P("rep", None),
            P("rep", "grp"),
            P(None, "rep", "grp"),
        ),
        out_specs=P(None, "rep", "grp"),
        check_vma=False,
    )
```

```python
import functools

import jax
import jax.numpy as jnp
from jax import lax
from jax.experimental import pallas as pl
from jax.experimental.pallas import tpu as pltpu
from jax.sharding import PartitionSpec as P

DAMPING = 0.1
MESH = pl.DeviceIdType.MESH
NX, NZ, NY, NL, NC = 4, 4, 4, 2, 2
NEAR = NY * NL
FIXED_OWNER = 15
CHUNKS = 8
SLACK = 2
FLIGHT = 4
LAG = 1
READY = CHUNKS + 3 * SLACK + 1
ROWS = 256 // CHUNKS
WIDE = 1024 + 128
BF16, F32, I16 = jnp.bfloat16, jnp.float32, jnp.int16


def coords():
    rep, grp = lax.axis_index("rep"), lax.axis_index("grp")
    return rep // NZ, rep % NZ, grp // (NL * NC), (grp // NC) % NL, grp % NC


def dev(x, zh, y, zl, c):
    return (x * NZ + zh, y * (NL * NC) + zl * NC + c)


def remote(src, dst, ss, rs, to):
    return pltpu.make_async_remote_copy(src_ref=src, dst_ref=dst, send_sem=ss, recv_sem=rs, device_id=to, device_id_type=MESH)


def at(start, size):
    return pl.ds(pl.multiple_of(start, size), size)


def split(value):
    high = value.astype(BF16)
    low = (value - high.astype(F32)).astype(BF16)
    return jnp.concatenate([high, low], axis=0)


def fold(value):
    half = value.shape[0] // 2
    return value[:half] + value[half:]


def code(value):
    top = jnp.maximum(jnp.max(jnp.abs(value), axis=0, keepdims=True), 1e-30)
    scale = top * (1 / 32767)
    digits = jnp.round(value * (32767 / top)).astype(jnp.int32).astype(jnp.int16)
    return digits, jnp.concatenate([scale[:, :128], scale[:, 128:], jnp.zeros((6, 128), F32)], axis=0)


def decode(digits, tile):
    scale = jnp.concatenate([tile[0:1], tile[1:2]], axis=1)
    return digits.astype(jnp.int32).astype(F32) * scale


def dot(left, right, dims=((1,), (0,))):
    return lax.dot_general(left, right, (dims, ((), ())), preferred_element_type=F32)


def kernel(other, owners, store_a, sg, vals_a, vals_g, grads, out, piece, gt, gx, qg, qa, yt, ys, yr, yv, t4, mid, wt, wr, wc, ws, wall, wv, wf, mx, mc, ms, mv,
           orc, orv, rot, qg_ss, qg_rs, fw_ss, qa_ss, qa_rs, qf_ss, ga_ss, ga_rs, gx_ss, gx_rs, gc_ss, gc_rs, loc, y_ss, y_rs, s_ss, s_rs, t_ss, t_rs,
           w_ss, w_rs, a_ss, a_rs, v_ss, v_rs, c_ss, c_rs, o_ss, o_rs, p_ss, p_rs):
    x, zh, y, zl, c = coords()
    q = y * NL + zl

    def near(i):
        return (y + i // NL) % NY, (zl + i % NL) % NL

    barrier = pltpu.get_barrier_semaphore()

    def greet(peer):
        pl.semaphore_signal(barrier, inc=1, device_id=peer, device_id_type=MESH)

    @pl.loop(1, NX)
    def _(d):
        greet(dev((x + d) % NX, zh, y, zl, 0))
        greet(dev((x + d) % NX, zh, y, zl, 1))
        greet(dev(x, (zh + d) % NZ, y, zl, c))

    @pl.loop(1, NEAR)
    def _(i):
        ty, tl = near(i)
        greet(dev(x, zh, ty, tl, 0))
        greet(dev(x, zh, ty, tl, 1))

    greet(dev(x, zh, y, zl, 1 - c))

    first = owners[0] == FIXED_OWNER
    gt[0] = jnp.where(first, grads[0], grads[1])
    gt[1] = jnp.where(first, grads[1], grads[0])

    def source(layer):
        return [layer * (other // NZ) + (1 - layer) * (FIXED_OWNER // NZ), layer * (other % NZ) + (1 - layer) * (FIXED_OWNER % NZ)]

    def mine(layer):
        return (x == source(layer)[0]) & (zh == source(layer)[1])

    owner = mine(0) | mine(1)
    owned = jnp.where(mine(1), 1, 0)

    grp = q * NC + c

    @pl.when(owner)
    def _():
        load = pltpu.make_async_copy(store_a.at[0, at(((grp % 4) * 4 + grp // 4) * 64, 64), :], piece.at[:, pl.ds(0, 1024)], loc.at[0])
        load.start()
        va, vg = vals_a[...].astype(F32), vals_g[...].astype(F32)
        lines = [va[:, i * 128:(i + 1) * 128] for i in range(8)] + [vg[:, i * 128:(i + 1) * 128] for i in range(2)]
        piece[:, 1024:WIDE] = jnp.concatenate(lines + [jnp.zeros((54, 128), F32)], axis=0).astype(BF16)
        load.wait()

    pl.semaphore_wait(barrier, 3 * (NX - 1) + 2 * (NEAR - 1) + 1)

    def qa_first(d):
        tx = (x + d) % NX
        return remote(piece.at[at(tx * 16, 16), :], qa.at[y, zl, c, tx], qa_ss.at[d], qa_rs.at[c], dev(tx, zh, y, zl, owned))

    def qg_first(k, d, core):
        tx = (x + d) % NX
        return remote(sg.at[0, at(k * ROWS, ROWS), at((tx * NC + core) * 512, 512)], qg.at[owned, at(c * 256 + k * ROWS, ROWS), :],
                      qg_ss.at[k, d, core], qg_rs.at[owned, c, k], dev(tx, zh, y, zl, core))

    def qg_sent(k):
        @pl.loop(0, (NX - 1) * NC)
        def _(i):
            qg_first(k, i // NC + 1, i % NC).wait_send()
        qg_first(k, 0, 1 - c).wait_send()

    def qg_local(k):
        return pltpu.make_async_copy(sg.at[0, at(k * ROWS, ROWS), at((x * NC + c) * 512, 512)],
                                     qg.at[owned, at(c * 256 + k * ROWS, ROWS), :], qg_rs.at[owned, c, k])

    tile = at(x * 64, 64), at(c * 256, 256)

    def g_x(l, d):
        return remote(gt.at[l], gx.at[l, tile[0], tile[1]], gx_ss.at[l, d], gx_rs.at[l, d], dev((x + d) % NX, zh, y, zl, c))

    def g_c(l):
        half = gx.at[l, :, tile[1]]
        return remote(half, half, gc_ss.at[l], gc_rs.at[l], dev(x, zh, y, zl, 1 - c))

    @pl.when(owner)
    def _():
        @pl.loop(1, NX)
        def _(d):
            qa_first(d).start()

        @pl.when(c == owned)
        def _():
            pltpu.make_async_copy(piece.at[at(x * 16, 16), :], qa.at[y, zl, c, x], qa_rs.at[c]).start()

        @pl.when(c != owned)
        def _():
            qa_first(0).start()

    def ring(layer, part):
        oz = source(layer)[1]
        return (zh + 1 + 2 * part) % NZ, (1 - part) * ((zh + NZ - oz) % NZ) + part * ((oz + NZ - zh) % NZ)

    def qa_on(part):
        block = qa.at[y, zl, part, x]
        return remote(block, block, qf_ss.at[part], qa_rs.at[part], dev(x, ring(c, part)[0], y, zl, c))

    def qg_on(layer, part, k):
        block = qg.at[layer, at(part * 256 + k * ROWS, ROWS), :]
        return remote(block, block, fw_ss.at[layer, part, k], qg_rs.at[layer, part, k], dev(x, ring(layer, part)[0], y, zl, c))

    def over_x(block, stage, act):
        @pl.loop(1, NX)
        def _(d):
            act(remote(block, block, ga_ss.at[stage, d], ga_rs.at[stage, d], dev((x + d) % NX, zh, y, zl, c)))

    def over_y(block, stage, act):
        @pl.loop(1, NY)
        def _(d):
            act(remote(block, block, ga_ss.at[stage, d], ga_rs.at[stage, d], dev(x, zh, (y + d) % NY, zl, c)))

    def over_zl(block, stage, act):
        act(remote(block, block, ga_ss.at[stage, 0], ga_rs.at[stage, 0], dev(x, zh, y, 1 - zl, c)))

    stages = (
        (lambda act: over_zl(qa.at[y, zl, :, x], 0, act), lambda act: over_y(qa.at[y, :, :, x], 1, act),
         lambda act: over_x(qa.at[:, :, :, x], 2, act)),
        (lambda act: over_x(qa.at[y, zl, :, x], 0, act), lambda act: over_zl(qa.at[y, zl], 1, act),
         lambda act: over_y(qa.at[y], 2, act)),
    )

    def gather(stage, act):
        for core in range(NC):
            @pl.when(c == core)
            def _():
                stages[core][stage](act)

    def begin(copy):
        copy.start()

    def arrived(copy):
        copy.wait_recv()

    def left(copy):
        copy.wait_send()

    def y_copy(l, i):
        ty, tl = near(i)
        tq = ty * NL + tl
        return [remote(yt.at[l, tq], yr.at[q, c], y_ss.at[l, i], y_rs.at[i, c], dev(x, zh, ty, tl, l)),
                remote(ys.at[l, tq], yv.at[q, c], s_ss.at[l, i], s_rs.at[i, c], dev(x, zh, ty, tl, l))]

    @pl.loop(0, READY + LAG + 1)
    def _(t):
        @pl.when(owner & (t < CHUNKS))
        def _():
            @pl.when(t >= FLIGHT)
            def _():
                qg_sent(t - FLIGHT)

            @pl.loop(0, (NX - 1) * NC)
            def _(i):
                qg_first(t, (i // NC + 1) % 3 + 1, i % NC).start()
            qg_first(t, 0, 1 - c).start()
            qg_local(t).start()

        @pl.loop(0, 2)
        def _(part):
            away = ring(c, part)[1]

            @pl.when(away * SLACK == t)
            def _():
                qa_on(part).wait_recv()

                @pl.when(away < NZ - 1)
                def _():
                    qa_on(part).start()

        @pl.loop(0, 4)
        def _(flow):
            layer, part = flow // 2, flow % 2
            away = ring(layer, part)[1]
            k = t - 1 - SLACK * away - LAG * layer

            @pl.when((k >= 0) & (k < CHUNKS))
            def _():
                qg_on(layer, part, k).wait_recv()

                @pl.when(away < NZ - 1)
                def _():
                    @pl.when(k >= FLIGHT)
                    def _():
                        qg_on(layer, part, k - FLIGHT).wait_send()
                    qg_on(layer, part, k).start()

        @pl.when(t == 8)
        def _():
            @pl.loop(0, 2)
            def _(l):
                @pl.loop(1, NX)
                def _(d):
                    g_x(l, d).start()
                gx[l, tile[0], tile[1]] = gt[l]

        for stage, when in enumerate((7, 8, 9)):
            @pl.when(t == when)
            def _():
                if stage:
                    gather(stage - 1, arrived)
                gather(stage, begin)

        @pl.when(t == READY - 1)
        def _():
            @pl.loop(0, 2)
            def _(l):
                @pl.loop(1, NX)
                def _(d):
                    g_x(l, d).wait_recv()
                g_c(l).start()

        @pl.when((t == READY) | (t == READY + LAG))
        def _():
            l = (t - READY) // LAG
            g_c(l).wait_recv()
            both = split(gx[l])

            @pl.loop(0, 4)
            def _(h):
                part = fold(dot(both, qg[l, :, at(h * 128, 128)])).T
                for k in range(2):
                    yt[l, h * 2 + k], ys[l, h * 2 + k] = code(part[k * 64:(k + 1) * 64])

            @pl.loop(1, NEAR)
            def _(i):
                for copy in y_copy(l, i):
                    copy.start()

            @pl.when(c == l)
            def _():
                yr[q, l] = yt[l, q]
                yv[q, l] = ys[l, q]

            @pl.when(c != l)
            def _():
                for copy in y_copy(l, 0):
                    copy.start()

    def y_wait(i, k):
        sq = ((y + NY - i // NL) % NY) * NL + (zl + i % NL) % NL
        remote(yr.at[sq, k], yr.at[sq, k], y_ss.at[0, i], y_rs.at[i, k], dev(x, zh, y, zl, 1 - c)).wait_recv()
        remote(yv.at[sq, k], yv.at[sq, k], s_ss.at[0, i], s_rs.at[i, k], dev(x, zh, y, zl, 1 - c)).wait_recv()

    y_wait(0, 1 - c)

    @pl.loop(1, NEAR)
    def _(i):
        for k in range(NC):
            y_wait(i, k)

    @pl.loop(0, NC)
    def _(k):
        t4[at(k * 64, 64), :] = lax.fori_loop(0, NEAR, lambda i, total: total + decode(yr[i, k], yv[i, k]), jnp.zeros((64, 256), F32))

    def t_copy(d):
        to = (zh + d) % NZ
        return remote(t4.at[at(to * 32, 32), :], mid.at[zh], t_ss.at[d], t_rs.at[d], dev(x, to, y, zl, c))

    @pl.loop(1, NZ)
    def _(d):
        t_copy(d).start()

    mid[zh] = t4[at(zh * 32, 32), :]

    for stage in range(2):
        gather(stage, left)

    @pl.loop(0, 2)
    def _(part):
        @pl.when(ring(c, part)[1] < NZ - 1)
        def _():
            qa_on(part).wait_send()

    @pl.loop(0, 4)
    def _(flow):
        layer, part = flow // 2, flow % 2

        @pl.when(ring(layer, part)[1] < NZ - 1)
        def _():
            @pl.loop(CHUNKS - FLIGHT, CHUNKS)
            def _(k):
                qg_on(layer, part, k).wait_send()

    @pl.when(owner)
    def _():
        @pl.loop(1, NX)
        def _(d):
            qa_first(d).wait_send()

        @pl.when(c != owned)
        def _():
            qa_first(0).wait_send()

        @pl.loop(CHUNKS - FLIGHT, CHUNKS)
        def _(k):
            qg_sent(k)

    @pl.loop(1, NZ)
    def _(d):
        t_copy(d).wait_recv()

    gather(2, arrived)

    spec_a = jnp.concatenate([qa[0, 0, 0, 0, :, 1024:WIDE].astype(F32)[i:i + 1] for i in range(8)], axis=1)
    spot = (x * 2 + zh // 2) * 2 + q // 4
    line = qa[spot // 4, (spot // 2) % 2, spot % 2, 0, :, 1024:WIDE].astype(F32)
    line = jnp.concatenate([line[8:9], line[9:10]], axis=1)
    start = (q % 4) * 64 + (zh % 2) * 32
    pick = lax.broadcasted_iota(jnp.int32, (32, 256), 1) == lax.broadcasted_iota(jnp.int32, (32, 256), 0) + start
    spec_g = jnp.sum(jnp.where(pick, line, 0.0), axis=1, keepdims=True)
    turned = split(jnp.concatenate([mid[k] for k in range(NZ)], axis=1))

    @pl.loop(0, 4)
    def _(k):
        rot[k] = fold(dot(turned, qa[:, :, :, :, :, at(k * 256, 256)].reshape(1024, 256)))

    rotated = jnp.concatenate([rot[k] for k in range(4)], axis=1)
    scaled = split(rotated / (spec_g * spec_a + DAMPING))

    @pl.loop(0, 4)
    def _(k):
        wt[k] = fold(dot(scaled, qa[k, :, :, :, :, 0:1024].reshape(256, 1024), ((1,), (1,))))

    def w_copy(d):
        to = (zh + d) % NZ
        return remote(wt.at[to], wr.at[at(zh * 32, 32), :], w_ss.at[d], w_rs.at[d], dev(x, to, y, zl, c))

    @pl.loop(1, NZ)
    def _(d):
        w_copy(d).start()

    wr[at(zh * 32, 32), :] = wt[zh]

    @pl.loop(0, 2)
    def _(l):
        @pl.loop(1, NEAR)
        def _(i):
            for copy in y_copy(l, i):
                copy.wait_send()
    for copy in y_copy(1 - c, 0):
        copy.wait_send()

    @pl.loop(1, NZ)
    def _(d):
        w_copy(d).wait_recv()

    def a_copy(k, i):
        ty, tl = near(i)
        return [remote(wc.at[k], wall.at[c, q], a_ss.at[k, i], a_rs.at[c, i], dev(x, zh, ty, tl, k)),
                remote(ws.at[k], wv.at[c, q], v_ss.at[k, i], v_rs.at[c, i], dev(x, zh, ty, tl, k))]

    for k in range(NC):
        wc[k], ws[k] = code(wr[k * 64:(k + 1) * 64, :])

    @pl.loop(1, NEAR)
    def _(i):
        for k in range(NC):
            for copy in a_copy(k, i):
                copy.start()
    for copy in a_copy(1 - c, 0):
        copy.start()
    wall[c, q] = wc[c]
    wv[c, q] = ws[c]

    def c_copy(l):
        return remote(mx.at[l, 1 - c], mc.at[l], c_ss.at[l], c_rs.at[l], dev(x, zh, y, zl, 1 - c))

    def o_copy(l, d):
        to = (x + d) % NX
        return [remote(ms.at[l, to], orc.at[l, x], o_ss.at[l, d], o_rs.at[l, d], dev(to, zh, y, zl, c)),
                remote(mv.at[l, to], orv.at[l, x], p_ss.at[l, d], p_rs.at[l, d], dev(to, zh, y, zl, c))]

    def a_wait(l, i):
        sq = ((y + NY - i // NL) % NY) * NL + (zl + i % NL) % NL
        remote(wall.at[l, sq], wall.at[l, sq], a_ss.at[0, i], a_rs.at[l, i], dev(x, zh, y, zl, 1 - c)).wait_recv()
        remote(wv.at[l, sq], wv.at[l, sq], v_ss.at[0, i], v_rs.at[l, i], dev(x, zh, y, zl, 1 - c)).wait_recv()

    @pl.loop(0, 2)
    def _(l):
        @pl.when(c != l)
        def _():
            a_wait(l, 0)

        @pl.loop(1, NEAR)
        def _(i):
            a_wait(l, i)

        @pl.loop(0, NEAR)
        def _(i):
            wf[at(i * 64, 64), :] = decode(wall[l, i], wv[l, i])
        both = split(wf[...].T)

        @pl.loop(0, 2)
        def _(h):
            mx[l, h] = fold(dot(both, qg[l, at(h * 256, 256), :], ((1,), (1,))))
        c_copy(l).start()

    @pl.loop(0, 2)
    def _(l):
        c_copy(l).wait_recv()

        @pl.loop(0, NX)
        def _(k):
            ms[l, k], mv[l, k] = code(mx[l, c, at(k * 64, 64), :] + mc[l, at(k * 64, 64), :])

        @pl.loop(1, NX)
        def _(d):
            for copy in o_copy(l, d):
                copy.start()
        orc[l, x] = ms[l, x]
        orv[l, x] = mv[l, x]

    @pl.loop(0, 2)
    def _(l):
        @pl.loop(1, NX)
        def _(d):
            for copy in o_copy(l, d):
                copy.wait_recv()
        out[l] = lax.fori_loop(0, NX, lambda i, total: total + decode(orc[l, i], orv[l, i]), jnp.zeros((64, 256), F32))

    @pl.loop(0, 2)
    def _(l):
        @pl.loop(1, NEAR)
        def _(i):
            for copy in a_copy(l, i):
                copy.wait_send()
        c_copy(l).wait_send()
        g_c(l).wait_send()

        @pl.loop(1, NX)
        def _(d):
            for copy in o_copy(l, d):
                copy.wait_send()
            g_x(l, d).wait_send()
    for copy in a_copy(1 - c, 0):
        copy.wait_send()

    @pl.loop(1, NZ)
    def _(d):
        t_copy(d).wait_send()
        w_copy(d).wait_send()
    gather(2, left)


def run(other, owners, store_a, store_g, vals_a, vals_g, grads):
    dma = pltpu.SemaphoreType.DMA
    vmem, anywhere = pl.BlockSpec(memory_space=pltpu.VMEM), pl.BlockSpec(memory_space=pl.ANY)
    return pl.pallas_call(
        functools.partial(kernel, other),
        out_shape=jax.ShapeDtypeStruct((2, 64, 256), F32),
        in_specs=[pl.BlockSpec(memory_space=pltpu.SMEM), anywhere, anywhere, vmem, vmem, vmem],
        out_specs=vmem,
        scratch_shapes=[
            pltpu.VMEM((64, WIDE), BF16),
            pltpu.VMEM((2, 64, 256), F32),
            pltpu.VMEM((2, 256, 512), F32),
            pltpu.VMEM((2, 512, 512), BF16),
            pltpu.VMEM((NY, NL, NC, NX, 16, WIDE), BF16),
            pltpu.VMEM((2, NEAR, 64, 256), I16),
            pltpu.VMEM((2, NEAR, 8, 128), F32),
            pltpu.VMEM((NEAR, 2, 64, 256), I16),
            pltpu.VMEM((NEAR, 2, 8, 128), F32),
            pltpu.VMEM((128, 256), F32),
            pltpu.VMEM((4, 32, 256), F32),
            pltpu.VMEM((4, 32, 256), F32),
            pltpu.VMEM((128, 256), F32),
            pltpu.VMEM((2, 64, 256), I16),
            pltpu.VMEM((2, 8, 128), F32),
            pltpu.VMEM((2, NEAR, 64, 256), I16),
            pltpu.VMEM((2, NEAR, 8, 128), F32),
            pltpu.VMEM((512, 256), F32),
            pltpu.VMEM((2, 2, 256, 256), F32),
            pltpu.VMEM((2, 256, 256), F32),
            pltpu.VMEM((2, 4, 64, 256), I16),
            pltpu.VMEM((2, 4, 8, 128), F32),
            pltpu.VMEM((2, 4, 64, 256), I16),
            pltpu.VMEM((2, 4, 8, 128), F32),
            pltpu.VMEM((4, 32, 256), F32),
            dma((CHUNKS, NX, NC)), dma((2, NC, CHUNKS)), dma((2, 2, CHUNKS)),
            dma((NX,)), dma((2,)), dma((2,)), dma((3, 4)), dma((3, 4)),
            dma((2, 4)), dma((2, 4)), dma((2,)), dma((2,)), dma((1,)),
            dma((2, 8)), dma((8, 2)), dma((2, 8)), dma((8, 2)), dma((4,)), dma((4,)), dma((4,)), dma((4,)),
            dma((2, 8)), dma((2, 8)), dma((2, 8)), dma((2, 8)),
            dma((2,)), dma((2,)), dma((2, 4)), dma((2, 4)), dma((2, 4)), dma((2, 4)),
        ],
        compiler_params=pltpu.CompilerParams(collective_id=other, has_side_effects=True, vmem_limit_bytes=40 * 2**20),
        name=f"kfac_{other}",
    )(owners, store_a, store_g, vals_a, vals_g, grads)


def local(owners, store_a, store_g, vals_a, vals_g, grads):
    first = owners[0] == FIXED_OWNER
    other = jnp.where(first, owners[1], owners[0])
    variants = [functools.partial(run, k) for k in range(FIXED_OWNER)]
    result = lax.switch(other, variants, owners, store_a, store_g, vals_a, vals_g, grads)
    return jnp.where(first, result, result[::-1])


def solution(mesh):
    return jax.shard_map(
        local,
        mesh=mesh,
        in_specs=(
            P(),
            P("rep", None, None),
            P("rep", "grp", None),
            P("rep", None),
            P("rep", "grp"),
            P(None, "rep", "grp"),
        ),
        out_specs=P(None, "rep", "grp"),
        check_vma=False,
    )
```
